32 devices in a mesh: ctx: 8 (over y, x, core), tp: 4 (over z).
Axes of the slice: x: 2, y: 2, z: 4, core: 2. Of those that a mesh axis runs over, the one named last changes fastest.
Arguments:
- query_gate: bfloat16 [16, 524288], P('tp', 'ctx'), may hold values from -6 to 6
- key_branch: bfloat16 [16, 524288], P('tp', 'ctx'), may hold values from -6 to 6
- value_branch: bfloat16 [16, 524288], P('tp', 'ctx'), may hold values from -6 to 6
- long_filter: float32 [16, 524288], P('tp', 'ctx'), may hold values from -0.0078125 to 0.0078125
- skip_gain: float32 [16], P('tp'), may hold values from 0.5 to 1.5
- out_weight: bfloat16 [16, 16], replicated, may hold values from -1.5 to 1.5
Outputs:
- mixed: bfloat16 [16, 524288], P('tp', 'ctx')
The draws below stay inside these ranges and needn't reach their ends.
All inputs are finite; a program needn't handle non-finite values.
Results may differ from the reference program's by a relative error of at most 0.02.
Values may be sent and summed in bfloat16 or wider, within the bound.
No kernel may reach another device: no remote copies, remote signals or barrier semaphores. Data moves between devices by JAX's collectives and lax.ppermute only.
A program may use at most 256 MiB of HBM per device.

```python
import jax
import jax.numpy as jnp

SEQ = 524288
CHANNELS = 16


def levels(stream_key, shape, split, low, largest):
    factor_of, own = 1.0, jax.random.fold_in(stream_key, 6)
    for dim, shards_of in split:
        steps = jnp.exp(jax.random.uniform(jax.random.fold_in(own, dim), (shards_of,), jnp.float32, low / len(split), largest / len(split)))
        factor_of = factor_of * jnp.repeat(steps, shape[dim] // shards_of).reshape([-1 if axis == dim else 1 for axis in range(len(shape))])
    return factor_of


def bell_draw(own_key, dims, spread, most, split=(), kind=jnp.bfloat16):
    factor_of = levels(own_key, dims, split, -0.22, 0.18) if split else 1.0
    entries = jax.random.normal(own_key, dims, jnp.float32) * spread * factor_of
    return jnp.minimum(jnp.maximum(entries, -most), most).astype(kind)


def setup_inputs(seed: int = 0) -> dict:
    key_of = jax.random.split(jax.random.key(seed), 7)
    return {
        "query_gate": bell_draw(key_of[0], (CHANNELS, SEQ), 1.0, 6.0, ((0, 4), (1, 8))),
        "key_branch": bell_draw(key_of[1], (CHANNELS, SEQ), 1.0, 6.0, ((0, 4), (1, 8))),
        "value_branch": bell_draw(key_of[2], (CHANNELS, SEQ), 1.0, 6.0, ((0, 4), (1, 8))),
        "long_filter": bell_draw(key_of[3], (CHANNELS, SEQ), SEQ ** -0.5, 0.0078125, ((0, 4), (1, 8)), jnp.float32),
        "skip_gain": jnp.clip(0.5 + 1.0 * jax.random.uniform(key_of[4], (CHANNELS,), jnp.float32) ** levels(key_of[4], (CHANNELS,), ((0, 4),), -0.2, 0.2), 0.5, 1.5),
        "out_weight": bell_draw(key_of[5], (CHANNELS, CHANNELS), CHANNELS ** -0.5, 1.5),
    }


def reference(query_gate, key_branch, value_branch, long_filter, skip_gain, out_weight):
    signal = key_branch.astype(jnp.float32) * value_branch.astype(jnp.float32)
    fft_length = 2 * SEQ
    signal_spec = jnp.fft.rfft(signal, n=fft_length, axis=1)
    filter_spec = jnp.fft.rfft(long_filter, n=fft_length, axis=1)
    conv = jnp.fft.irfft(signal_spec * filter_spec, n=fft_length, axis=1)[:, :SEQ]
    gated = (query_gate.astype(jnp.float32) * (conv + skip_gain[:, None] * signal)).astype(jnp.bfloat16)
    mixed = jnp.dot(out_weight.T, gated, preferred_element_type=jnp.float32)
    return mixed.astype(jnp.bfloat16)
```

```python
import functools

import jax
import jax.numpy as jnp
import numpy as np
from jax import lax
from jax.experimental import pallas as pl
from jax.experimental.pallas import tpu as pltpu
from jax.sharding import PartitionSpec as P

COLS = 512
CHUNKS = 2
BF = jnp.bfloat16
F32 = jnp.float32
VMEM = pl.BlockSpec(memory_space=pltpu.VMEM)
SMEM = pl.BlockSpec(memory_space=pltpu.SMEM)


def make_tables(ctx_count, group, chans, rows):
    big = ctx_count * rows
    own = big // group
    length = big * COLS
    k_one = np.arange(big, dtype=np.int64)
    n_one = np.arange(big, dtype=np.int64)
    angle = 2 * np.pi / (4 * big) * ((4 * k_one[:, None] + 1) * n_one[None, :] % (4 * big))
    both = np.stack([np.cos(angle), -np.sin(angle)], 0)
    both = both.reshape(2, group, own, chans, group, rows)
    left = np.empty((group, group, 2 * own, chans * rows))
    for sub in range(group):
        for step in range(group):
            left[sub, step] = both[:, sub, :, :, (sub + step) % group].reshape(2 * own, -1)
    n_two = np.arange(COLS, dtype=np.int64)
    angle = 2 * np.pi / (4 * length) * ((4 * k_one[:, None] + 1) * n_two[None, :] % (4 * length))
    turn = np.stack([np.cos(angle), -np.sin(angle)], 0).reshape(2, group, own, COLS)
    turn = turn.transpose(1, 0, 2, 3)
    angle = 2 * np.pi / COLS * (n_two[:, None] * n_two[None, :] % COLS)
    cos, sin = np.cos(angle), np.sin(angle)
    right = np.block([[cos, -sin], [sin, cos]])
    bf = jnp.bfloat16
    return (
        left.astype(bf),
        np.ascontiguousarray(left.transpose(0, 1, 3, 2)).astype(bf),
        np.ascontiguousarray(turn).astype(np.float32),
        right.astype(bf),
        np.ascontiguousarray(right.T).astype(bf),
    )


def dot(left, right):
    return jnp.dot(left, right, preferred_element_type=F32)


def forward(parts, left_ref, turn_ref, right_ref, mid_ref):
    own = mid_ref.shape[0]
    total = dot(left_ref[0], parts[0][...])
    for step in range(1, len(parts)):
        total += dot(left_ref[step], parts[step][...])
    val_re, val_im = total[:own], total[own:]
    tab_re, tab_im = turn_ref[0], turn_ref[1]
    mid_ref[:, :COLS] = (val_re * tab_re - val_im * tab_im).astype(BF)
    mid_ref[:, COLS:] = (val_re * tab_im + val_im * tab_re).astype(BF)
    return dot(mid_ref[...], right_ref[...])


def filter_kernel(group, scale, sub_ref, *refs):
    parts, (left_ref, turn_ref, right_ref, out_ref, mid_ref) = refs[:group], refs[group:]
    out_ref[...] = forward(parts, left_ref, turn_ref, right_ref, mid_ref) * scale


def signal_kernel(group, sub_ref, *refs):
    parts = refs[:group]
    spec_ref, left_ref, turn_ref, right_ref, back_right_ref, back_left_ref = refs[group : group + 6]
    own_ref, send_ref, mid_ref, last_ref = refs[group + 6 :]
    own = mid_ref.shape[0]
    spec = forward(parts, left_ref, turn_ref, right_ref, mid_ref)
    sig_re, sig_im = spec[:, :COLS], spec[:, COLS:]
    fil_re, fil_im = spec_ref[:, :COLS], spec_ref[:, COLS:]
    mid_ref[:, :COLS] = (sig_re * fil_re - sig_im * fil_im).astype(BF)
    mid_ref[:, COLS:] = (sig_re * fil_im + sig_im * fil_re).astype(BF)
    back = dot(mid_ref[...], back_right_ref[...])
    val_re, val_im = back[:, :COLS], back[:, COLS:]
    tab_re, tab_im = turn_ref[0], turn_ref[1]
    last_ref[:own] = (val_re * tab_re + val_im * tab_im).astype(BF)
    last_ref[own:] = (val_im * tab_re - val_re * tab_im).astype(BF)
    own_ref[...] = dot(back_left_ref[0], last_ref[...])
    for step in range(1, group):
        send_ref[step - 1] = dot(back_left_ref[step], last_ref[...]).astype(BF)


def by_sub(shape):
    rank = len(shape)
    return pl.BlockSpec((None,) + shape, lambda i, sub: (sub[0],) + (0,) * rank)


def whole(shape):
    rank = len(shape)
    return pl.BlockSpec(shape, lambda i, sub: (0,) * rank)


def run_filter(sub, parts, left, turn, right, scale):
    group = len(parts)
    own = left.shape[2] // 2
    return pl.pallas_call(
        functools.partial(filter_kernel, group, scale),
        out_shape=jax.ShapeDtypeStruct((own, 2 * COLS), F32),
        grid_spec=pltpu.PrefetchScalarGridSpec(
            num_scalar_prefetch=1,
            grid=(1,),
            in_specs=[whole(part.shape) for part in parts]
            + [by_sub(left.shape[1:]), by_sub(turn.shape[1:]), whole(right.shape)],
            out_specs=whole((own, 2 * COLS)),
            scratch_shapes=[pltpu.VMEM((own, 2 * COLS), BF)],
        ),
        compiler_params=pltpu.CompilerParams(vmem_limit_bytes=50 * 2**20),
        name="filter_spectrum",
    )(sub, *parts, left, turn, right)


def run_signal(sub, parts, spec, left, turn, right, back_right, back_left):
    group = len(parts)
    own = left.shape[2] // 2
    half = left.shape[3]
    return pl.pallas_call(
        functools.partial(signal_kernel, group),
        out_shape=(
            jax.ShapeDtypeStruct((half, COLS), F32),
            jax.ShapeDtypeStruct((group - 1, half, COLS), BF),
        ),
        grid_spec=pltpu.PrefetchScalarGridSpec(
            num_scalar_prefetch=1,
            grid=(1,),
            in_specs=[whole(part.shape) for part in parts]
            + [whole(spec.shape), by_sub(left.shape[1:]), by_sub(turn.shape[1:])]
            + [whole(right.shape), whole(back_right.shape), by_sub(back_left.shape[1:])],
            out_specs=(whole((half, COLS)), whole((group - 1, half, COLS))),
            scratch_shapes=[
                pltpu.VMEM((own, 2 * COLS), BF),
                pltpu.VMEM((2 * own, COLS), BF),
            ],
        ),
        compiler_params=pltpu.CompilerParams(vmem_limit_bytes=56 * 2**20),
        name="signal_convolution",
    )(sub, *parts, spec, left, turn, right, back_right, back_left)


def mix_kernel(chans, plane_ref, weight_ref, own_ref, mid_ref, far_ref, edge_ref, acc_ref, out_ref):
    slots = (own_ref, mid_ref, far_ref, edge_ref)
    outs = acc_ref.shape[0]
    final_col = plane_ref[0] * outs
    part_col = plane_ref[3] * outs

    @pl.loop(0, own_ref.shape[1] // 16)
    def _(index):
        rows = pl.ds(pl.multiple_of(index * 16, 16), 16)
        acc = [None] * outs
        part = [None] * outs
        for slot, ref in enumerate(slots):
            for chan in range(chans):
                value = ref[chan, rows].astype(F32)
                row = plane_ref[slot] * chans + chan
                for feat in range(outs):
                    term = value * weight_ref[row, final_col + feat]
                    acc[feat] = term if acc[feat] is None else acc[feat] + term
                    if slot < 3:
                        term = value * weight_ref[row, part_col + feat]
                        part[feat] = term if part[feat] is None else part[feat] + term
        for feat in range(outs):
            acc_ref[feat, rows] = acc[feat]
            out_ref[feat, rows] = part[feat].astype(BF)


def run_mix(planes, weight, own, mid, far, edge):
    chans, rows, cols = own.shape
    outs = weight.shape[1] // 4
    return pl.pallas_call(
        functools.partial(mix_kernel, chans),
        out_shape=(
            jax.ShapeDtypeStruct((outs, rows, cols), F32),
            jax.ShapeDtypeStruct((outs, rows, cols), BF),
        ),
        in_specs=[SMEM, SMEM] + [VMEM] * 4,
        out_specs=(VMEM, VMEM),
        compiler_params=pltpu.CompilerParams(vmem_limit_bytes=32 * 2**20),
        name="mix_features",
    )(planes, weight, own, mid, far, edge)


def line_mix(gated, out_weight):
    plane = lax.axis_index("tp")
    near = plane < 2
    mid_of, far_of, edge_of = jnp.where(near, 2, 1), jnp.where(near, 3, 0), jnp.where(near, 0, 3)
    planes = jnp.stack([plane, mid_of, far_of, edge_of]).astype(jnp.int32)
    weight = out_weight.astype(F32)
    received = []
    for own in gated:
        mid = lax.ppermute(own, "tp", [(1, 2), (2, 1)])
        far = lax.ppermute(own, "tp", [(0, 2), (3, 1)])
        edge = lax.ppermute(own, "tp", [(0, 1), (3, 2)])
        received.append((own, mid, far, edge))
    sums = [run_mix(planes, weight, *slots) for slots in received]
    mixed = []
    for acc, send in sums:
        got = lax.ppermute(send, "tp", [(2, 3), (1, 0)])
        mixed.append((acc + got.astype(F32)).astype(BF))
    return mixed


def gather_mix(gated, out_weight):
    plane = lax.axis_index("tp")
    outs = out_weight.shape[1] // lax.axis_size("tp")
    own_cols = lax.dynamic_slice_in_dim(out_weight, plane * outs, outs, 1)
    return [
        jnp.einsum(
            "co,crl->orl",
            own_cols,
            lax.all_gather(own, "tp", axis=0, tiled=True),
            preferred_element_type=F32,
        ).astype(BF)
        for own in gated
    ]


def local(query_gate, key_branch, value_branch, long_filter, skip_gain, out_weight):
    ctx_count = lax.axis_size("ctx")
    ctx_index = lax.axis_index("ctx")
    chans, tok_count = query_gate.shape
    rows = tok_count // COLS
    group = ctx_count // chans
    length = ctx_count * tok_count
    sub = (ctx_index % group).astype(jnp.int32).reshape(1)
    shape = (chans, rows, COLS)
    left, back_left, turn, right, back_right = make_tables(ctx_count, group, chans, rows)
    swaps = [[sub_i + group * p for p in range(chans)] for sub_i in range(group)]

    def swap(value):
        return lax.all_to_all(value, "ctx", 0, 0, axis_index_groups=swaps, tiled=True)

    def shift(value, step):
        pairs = [
            (group * p + i, group * p + (i + step) % group)
            for p in range(chans)
            for i in range(group)
        ]
        return lax.ppermute(value, "ctx", pairs)

    def gather_parts(value):
        got = swap(value)
        parts = [got] + [shift(got, -step) for step in range(1, group)]
        return [part.reshape(chans * rows, COLS) for part in parts]

    filter_parts = gather_parts(long_filter.astype(BF).reshape(shape))
    product = key_branch.astype(F32) * value_branch.astype(F32)
    signal_parts = gather_parts(product.astype(BF).reshape(shape))
    spec = run_filter(sub, filter_parts, left, turn, right, 1.0 / length)
    conv, send = run_signal(sub, signal_parts, spec, left, turn, right, back_right, back_left)
    for step in range(1, group):
        conv += shift(send[step - 1], step).astype(F32)
    conv = conv.astype(BF).reshape(shape)
    query = query_gate.reshape(shape)
    key = key_branch.reshape(shape).astype(F32)
    value = value_branch.reshape(shape).astype(F32)
    size = rows // CHUNKS
    gated = []
    for chunk in range(CHUNKS):
        cut = slice(chunk * size, (chunk + 1) * size)
        got = swap(conv[:, cut]).astype(F32)
        skip = skip_gain[:, None, None] * (key[:, cut] * value[:, cut])
        gated.append((query[:, cut].astype(F32) * (got + skip)).astype(BF))
    mixed = (line_mix if lax.axis_size("tp") == 4 else gather_mix)(gated, out_weight)
    return jnp.concatenate(mixed, 1).reshape(-1, tok_count)


def solution(mesh):
    placed = (P("tp", "ctx"), P("tp", "ctx"), P("tp", "ctx"), P("tp", "ctx"), P("tp"), P())
    return jax.shard_map(
        local, mesh=mesh, in_specs=placed, out_specs=P("tp", "ctx"), check_vma=False
    )
```

```python
import functools

import jax
import jax.numpy as jnp
import numpy as np
from jax import lax
from jax.experimental import pallas as pl
from jax.experimental.pallas import tpu as pltpu
from jax.sharding import PartitionSpec as P

COLS = 512
CUTS = (0, 256, 512)
BF = jnp.bfloat16
F32 = jnp.float32
VMEM = pl.BlockSpec(memory_space=pltpu.VMEM)
SMEM = pl.BlockSpec(memory_space=pltpu.SMEM)
ANY = pl.BlockSpec(memory_space=pl.ANY)


def make_tables(ctx_count, group, chans, rows):
    big = ctx_count * rows
    own = big // group
    length = big * COLS
    k_one = np.arange(big, dtype=np.int64)
    n_one = np.arange(big, dtype=np.int64)
    angle = 2 * np.pi / (4 * big) * ((4 * k_one[:, None] + 1) * n_one[None, :] % (4 * big))
    both = np.stack([np.cos(angle), -np.sin(angle)], 0)
    both = both.reshape(2, group, own, chans, group, rows)
    left = np.empty((group, 2 * own, group, chans * rows))
    back_left = np.empty((group, chans * rows, group, 2 * own))
    for sub in range(group):
        for step in range(group):
            other = (sub + step) % group
            left[sub, :, step] = both[:, sub, :, :, other].reshape(2 * own, -1)
            back_left[sub, :, step] = both[:, other, :, :, sub].reshape(2 * own, -1).T
    n_two = np.arange(COLS, dtype=np.int64)
    angle = 2 * np.pi / (4 * length) * ((4 * k_one[:, None] + 1) * n_two[None, :] % (4 * length))
    turn = np.stack([np.cos(angle), -np.sin(angle)], 0).reshape(2, group, own, COLS)
    turn = np.ascontiguousarray(turn.transpose(1, 0, 2, 3))
    angle = 2 * np.pi / COLS * (n_two[:, None] * n_two[None, :] % COLS)
    cos, sin = np.cos(angle), np.sin(angle)
    right = np.block([[cos, -sin], [sin, cos]])
    return (
        left.reshape(group, 2 * own, big).astype(BF),
        back_left.reshape(group, chans * rows, 2 * big).astype(BF),
        turn.astype(np.float32),
        right.astype(BF),
        np.ascontiguousarray(right.T).astype(BF),
    )


def dot(left, right):
    return jnp.dot(left, right, preferred_element_type=F32)


def load(copies):
    started = [pltpu.make_async_copy(*copy) for copy in copies]
    for copy in started:
        copy.start()
    return started


def cost(flops, moved):
    return pl.CostEstimate(flops=flops, bytes_accessed=moved, transcendentals=0)


def params(mib):
    return pltpu.CompilerParams(vmem_limit_bytes=mib * 2**20)


def place():
    index = lax.axis_index("ctx")
    return index


def forward_stage(blocks, chans, group, x_ref, left_ref, turn_ref, mid_ref, waits):
    rows = blocks[0].shape[0]
    own = mid_ref.shape[0]
    home = lax.axis_index("ctx") // group
    for step in range(group):
        for rel in range(chans):
            first = pl.multiple_of((step * chans + (home ^ rel)) * rows, rows)
            x_ref[pl.ds(first, rows)] = blocks[step * chans + rel][...]
    waits[0].wait()
    for tile in range(0, COLS, 256):
        cut = slice(tile, tile + 256)
        val = dot(left_ref[...], x_ref[:, cut])
        if tile == 0:
            waits[1].wait()
        val_re, val_im = val[:own], val[own:]
        tab_re, tab_im = turn_ref[0, :, cut], turn_ref[1, :, cut]
        mid_ref[:, cut] = (val_re * tab_re - val_im * tab_im).astype(BF)
        cut_im = slice(COLS + tile, COLS + tile + 256)
        mid_ref[:, cut_im] = (val_re * tab_im + val_im * tab_re).astype(BF)


def back_stage(cols, prod, table_ref, turn_ref, out_ref):
    own = turn_ref.shape[1]
    for tile in range(cols[0], cols[1], 128):
        cut = slice(tile, tile + 128)
        dst = slice(tile - cols[0], tile - cols[0] + 128)
        val_re = dot(prod, table_ref[:, cut])
        val_im = dot(prod, table_ref[:, COLS + tile : COLS + tile + 128])
        tab_re, tab_im = turn_ref[0, :, cut], turn_ref[1, :, cut]
        out_ref[:own, dst] = (val_re * tab_re + val_im * tab_im).astype(BF)
        out_ref[own:, dst] = (val_im * tab_re - val_re * tab_im).astype(BF)


def filter_kernel(chans, group, scale, *refs):
    count = chans * group
    blocks, (left_hbm, turn_hbm, right_hbm, out_ref) = refs[:count], refs[count : count + 4]
    x_ref, left_ref, turn_ref, right_ref, mid_ref, sems = refs[count + 4 :]
    sub = lax.rem(lax.axis_index("ctx"), group)
    waits = load(
        [
            (left_hbm.at[sub], left_ref, sems.at[0]),
            (turn_hbm.at[sub], turn_ref, sems.at[1]),
            (right_hbm, right_ref, sems.at[2]),
        ]
    )
    forward_stage(blocks, chans, group, x_ref, left_ref, turn_ref, mid_ref, waits)
    waits[2].wait()
    for tile in range(0, 2 * COLS, 256):
        cut = slice(tile, tile + 256)
        out_ref[:, cut] = dot(mid_ref[...], right_ref[:, cut]) * scale


def signal_kernel(chans, group, cols, *refs):
    count = chans * group
    blocks = refs[:count]
    spec_ref, left_hbm, turn_hbm, right_hbm, back_hbm, prod_ref, out_ref = refs[count : count + 7]
    x_ref, left_ref, turn_ref, right_ref, back_ref, mid_ref, sems = refs[count + 7 :]
    sub = lax.rem(lax.axis_index("ctx"), group)
    waits = load(
        [
            (left_hbm.at[sub], left_ref, sems.at[0]),
            (turn_hbm.at[sub], turn_ref, sems.at[1]),
            (right_hbm, right_ref, sems.at[2]),
            (back_hbm, back_ref, sems.at[3]),
        ]
    )
    forward_stage(blocks, chans, group, x_ref, left_ref, turn_ref, mid_ref, waits)
    waits[2].wait()
    for tile in range(0, COLS, 256):
        cut, cut_im = slice(tile, tile + 256), slice(COLS + tile, COLS + tile + 256)
        sig_re = dot(mid_ref[...], right_ref[:, cut])
        sig_im = dot(mid_ref[...], right_ref[:, cut_im])
        fil_re, fil_im = spec_ref[:, cut], spec_ref[:, cut_im]
        prod_ref[:, cut] = (sig_re * fil_re - sig_im * fil_im).astype(BF)
        prod_ref[:, cut_im] = (sig_re * fil_im + sig_im * fil_re).astype(BF)
    waits[3].wait()
    back_stage(cols, prod_ref[...], back_ref, turn_ref, out_ref)


def later_kernel(group, cols, prod_ref, turn_hbm, back_hbm, out_ref, turn_ref, back_ref, sems):
    sub = lax.rem(lax.axis_index("ctx"), group)
    waits = load(
        [(back_hbm, back_ref, sems.at[0]), (turn_hbm.at[sub], turn_ref, sems.at[1])]
    )
    for wait in waits:
        wait.wait()
    back_stage(cols, prod_ref[...], back_ref, turn_ref, out_ref)


def position_kernel(chans, group, *refs):
    parts, table_hbm = refs[:group], refs[group]
    outs = refs[group + 1 : group + 1 + chans]
    table_ref, sum_ref, sems = refs[group + 1 + chans :]
    home = lax.axis_index("ctx") // group
    sub = lax.rem(lax.axis_index("ctx"), group)
    (wait,) = load([(table_hbm.at[sub], table_ref, sems.at[0])])
    wait.wait()
    depth = parts[0].shape[0]
    total = dot(table_ref[:, :depth], parts[0][...])
    for step in range(1, group):
        total += dot(table_ref[:, step * depth : (step + 1) * depth], parts[step][...])
    sum_ref[...] = total.astype(BF)
    rows = outs[0].shape[0]
    for rel in range(chans):
        outs[rel][...] = sum_ref[pl.ds(pl.multiple_of((home ^ rel) * rows, rows), rows)]


def gate_kernel(group, cols, *refs):
    chans = len(refs) - 5
    parts = refs[:chans]
    query_ref, key_ref, value_ref, gain_ref, out_ref = refs[chans:]
    home = lax.axis_index("ctx") // group
    cut = slice(*cols)
    for rel in range(chans):
        chan = home ^ rel
        signal = key_ref[chan, :, cut].astype(F32) * value_ref[chan, :, cut].astype(F32)
        total = parts[rel][...].astype(F32) + gain_ref[chan] * signal
        out_ref[chan] = (query_ref[chan, :, cut].astype(F32) * total).astype(BF)


def mix_kernel(chans, plane_ref, weight_ref, own_ref, mid_ref, far_ref, edge_ref, acc_ref, out_ref):
    slots = (own_ref, mid_ref, far_ref, edge_ref)
    outs = acc_ref.shape[0]
    final_col = plane_ref[0] * outs
    part_col = plane_ref[3] * outs

    @pl.loop(0, own_ref.shape[1] // 16)
    def _(index):
        rows = pl.ds(pl.multiple_of(index * 16, 16), 16)
        acc = [None] * outs
        part = [None] * outs
        for slot, ref in enumerate(slots):
            for chan in range(chans):
                value = ref[chan, rows].astype(F32)
                row = plane_ref[slot] * chans + chan
                for feat in range(outs):
                    term = value * weight_ref[row, final_col + feat]
                    acc[feat] = term if acc[feat] is None else acc[feat] + term
                    if slot < 3:
                        term = value * weight_ref[row, part_col + feat]
                        part[feat] = term if part[feat] is None else part[feat] + term
        for feat in range(outs):
            acc_ref[feat, rows] = acc[feat]
            out_ref[feat, rows] = part[feat].astype(BF)


def run_filter(blocks, chans, group, tables, scale):
    left, _, turn, right, _ = tables
    own, big = left.shape[1] // 2, left.shape[2]
    return pl.pallas_call(
        functools.partial(filter_kernel, chans, group, scale),
        out_shape=jax.ShapeDtypeStruct((own, 2 * COLS), F32),
        in_specs=[VMEM] * len(blocks) + [ANY] * 3,
        out_specs=VMEM,
        scratch_shapes=[
            pltpu.VMEM((big, COLS), BF),
            pltpu.VMEM(left.shape[1:], BF),
            pltpu.VMEM(turn.shape[1:], F32),
            pltpu.VMEM(right.shape, BF),
            pltpu.VMEM((own, 2 * COLS), BF),
            pltpu.SemaphoreType.DMA((3,)),
        ],
        compiler_params=params(24),
        cost_estimate=cost(4 * own * COLS * (big + 2 * COLS), 8 * 2**20),
        name="filter_spectrum",
    )(*blocks, left, turn, right)


def run_signal(blocks, spec, chans, group, tables, cols):
    left, _, turn, right, back = tables
    own, big = left.shape[1] // 2, left.shape[2]
    return pl.pallas_call(
        functools.partial(signal_kernel, chans, group, cols),
        out_shape=(
            jax.ShapeDtypeStruct((own, 2 * COLS), BF),
            jax.ShapeDtypeStruct((2 * own, cols[1] - cols[0]), BF),
        ),
        in_specs=[VMEM] * (len(blocks) + 1) + [ANY] * 4,
        out_specs=(VMEM, VMEM),
        scratch_shapes=[
            pltpu.VMEM((big, COLS), BF),
            pltpu.VMEM(left.shape[1:], BF),
            pltpu.VMEM(turn.shape[1:], F32),
            pltpu.VMEM(right.shape, BF),
            pltpu.VMEM(back.shape, BF),
            pltpu.VMEM((own, 2 * COLS), BF),
            pltpu.SemaphoreType.DMA((4,)),
        ],
        compiler_params=params(28),
        cost_estimate=cost(4 * own * COLS * (big + 4 * COLS), 12 * 2**20),
        name="signal_product",
    )(*blocks, spec, left, turn, right, back)


def run_later(prod, group, tables, cols):
    _, _, turn, _, back = tables
    own = prod.shape[0]
    return pl.pallas_call(
        functools.partial(later_kernel, group, cols),
        out_shape=jax.ShapeDtypeStruct((2 * own, cols[1] - cols[0]), BF),
        in_specs=[VMEM, ANY, ANY],
        out_specs=VMEM,
        scratch_shapes=[
            pltpu.VMEM(turn.shape[1:], F32),
            pltpu.VMEM(back.shape, BF),
            pltpu.SemaphoreType.DMA((2,)),
        ],
        compiler_params=params(16),
        cost_estimate=cost(8 * own * COLS * (cols[1] - cols[0]), 6 * 2**20),
        name="back_columns",
    )(prod, turn, back)


def run_position(parts, chans, group, tables):
    table = tables[1]
    out_rows, depth = table.shape[1:]
    cols = parts[0].shape[1]
    rows = out_rows // chans
    return pl.pallas_call(
        functools.partial(position_kernel, chans, group),
        out_shape=(jax.ShapeDtypeStruct((rows, cols), BF),) * chans,
        in_specs=[VMEM] * group + [ANY],
        out_specs=(VMEM,) * chans,
        scratch_shapes=[
            pltpu.VMEM(table.shape[1:], BF),
            pltpu.VMEM((out_rows, cols), BF),
            pltpu.SemaphoreType.DMA((1,)),
        ],
        compiler_params=params(20),
        cost_estimate=cost(2 * out_rows * depth * cols, 4 * 2**20),
        name="back_positions",
    )(*parts, table)


def run_gate(parts, query, key, value, gain, group, cols):
    chans, rows, _ = query.shape
    return pl.pallas_call(
        functools.partial(gate_kernel, group, cols),
        out_shape=jax.ShapeDtypeStruct((chans, rows, cols[1] - cols[0]), BF),
        in_specs=[VMEM] * (chans + 3) + [SMEM],
        out_specs=VMEM,
        compiler_params=params(12),
        cost_estimate=cost(4 * chans * rows * (cols[1] - cols[0]), 2 * 2**20),
        name="gate",
    )(*parts, query, key, value, gain)


def run_mix(planes, weight, own, mid, far, edge):
    chans, rows, cols = own.shape
    outs = weight.shape[1] // 4
    return pl.pallas_call(
        functools.partial(mix_kernel, chans),
        out_shape=(
            jax.ShapeDtypeStruct((outs, rows, cols), F32),
            jax.ShapeDtypeStruct((outs, rows, cols), BF),
        ),
        in_specs=[SMEM, SMEM] + [VMEM] * 4,
        out_specs=(VMEM, VMEM),
        compiler_params=params(12),
        cost_estimate=cost(56 * outs * rows * cols, 3 * 2**20),
        name="mix_features",
    )(planes, weight, own, mid, far, edge)


def line_mix(gated, out_weight):
    plane = lax.axis_index("tp")
    near = plane < 2
    mid_of, far_of, edge_of = jnp.where(near, 2, 1), jnp.where(near, 3, 0), jnp.where(near, 0, 3)
    planes = jnp.stack([plane, mid_of, far_of, edge_of]).astype(jnp.int32)
    weight = out_weight.astype(F32)
    mixed = []
    for own in gated:
        mid = lax.ppermute(own, "tp", [(1, 2), (2, 1)])
        far = lax.ppermute(own, "tp", [(0, 2), (3, 1)])
        edge = lax.ppermute(own, "tp", [(0, 1), (3, 2)])
        acc, send = run_mix(planes, weight, own, mid, far, edge)
        got = lax.ppermute(send, "tp", [(2, 3), (1, 0)])
        mixed.append((acc + got.astype(F32)).astype(BF))
    return mixed


def gather_mix(gated, out_weight):
    plane = lax.axis_index("tp")
    outs = out_weight.shape[1] // lax.axis_size("tp")
    own_cols = lax.dynamic_slice_in_dim(out_weight, plane * outs, outs, 1)
    return [
        jnp.einsum(
            "co,crl->orl",
            own_cols,
            lax.all_gather(own, "tp", axis=0, tiled=True),
            preferred_element_type=F32,
        ).astype(BF)
        for own in gated
    ]


def local(query_gate, key_branch, value_branch, long_filter, skip_gain, out_weight):
    ctx_count = lax.axis_size("ctx")
    chans, tok_count = query_gate.shape
    rows = tok_count // COLS
    group = ctx_count // chans
    length = ctx_count * tok_count
    home = lax.axis_index("ctx") // group
    shape = (chans, rows, COLS)
    tables = make_tables(ctx_count, group, chans, rows)

    def swap(values):
        got = [values[0]]
        for rel in range(1, chans):
            pairs = [
                (group * chip + core, group * (chip ^ rel) + core)
                for chip in range(chans)
                for core in range(group)
            ]
            got.append(lax.ppermute(values[rel], "ctx", pairs))
        return got

    def shift(value, step):
        pairs = [
            (group * chip + core, group * chip + (core + step) % group)
            for chip in range(chans)
            for core in range(group)
        ]
        return lax.ppermute(value, "ctx", pairs)

    def gather_blocks(value):
        relative = [lax.dynamic_index_in_dim(value, home ^ rel, 0, False) for rel in range(chans)]
        got = swap(relative)
        blocks = list(got)
        for step in range(1, group):
            blocks += [shift(part, -step) for part in got]
        return blocks

    filter_blocks = gather_blocks(long_filter.astype(BF).reshape(shape))
    query = query_gate.reshape(shape)
    key = key_branch.reshape(shape)
    value = value_branch.reshape(shape)
    signal_blocks = gather_blocks((key.astype(F32) * value.astype(F32)).astype(BF))
    spec = run_filter(filter_blocks, chans, group, tables, 1.0 / length)
    spans = list(zip(CUTS[:-1], CUTS[1:]))
    prod, first = run_signal(signal_blocks, spec, chans, group, tables, spans[0])
    gated = []
    for span in spans:
        back = first if span == spans[0] else run_later(prod, group, tables, span)
        parts = [back] + [shift(back, -step) for step in range(1, group)]
        got = swap(run_position(parts, chans, group, tables))
        gated.append(run_gate(got, query, key, value, skip_gain, group, span))
    mixed = (line_mix if lax.axis_size("tp") == 4 else gather_mix)(gated, out_weight)
    return jnp.concatenate(mixed, 2).reshape(-1, tok_count)


def solution(mesh):
    placed = (P("tp", "ctx"), P("tp", "ctx"), P("tp", "ctx"), P("tp", "ctx"), P("tp"), P())
    return jax.shard_map(
        local, mesh=mesh, in_specs=placed, out_specs=P("tp", "ctx"), check_vma=False
    )
```

```python
import functools

import jax
import jax.numpy as jnp
import numpy as np
from jax import lax
from jax.experimental import pallas as pl
from jax.experimental.pallas import tpu as pltpu
from jax.sharding import PartitionSpec as P

COLS = 512
STEP = 32
CUTS = (0, 256, 512)
BF = jnp.bfloat16
F32 = jnp.float32
VMEM = pl.BlockSpec(memory_space=pltpu.VMEM)
SMEM = pl.BlockSpec(memory_space=pltpu.SMEM)
HBM = pl.BlockSpec(memory_space=pltpu.HBM)


def make_tables(ctx_count, group, chans, rows):
    big = ctx_count * rows
    own = big // group
    length = big * COLS
    k_one = np.arange(big, dtype=np.int64)
    n_one = np.arange(big, dtype=np.int64)
    angle = 2 * np.pi / (4 * big) * ((4 * k_one[:, None] + 1) * n_one[None, :] % (4 * big))
    both = np.stack([np.cos(angle), -np.sin(angle)], 0)
    both = both.reshape(2, group, own, chans, group, rows)
    left = np.empty((group, 2 * own, group, chans * rows))
    back_left = np.empty((group, chans * rows, group, 2 * own))
    for sub in range(group):
        for step in range(group):
            other = (sub + step) % group
            left[sub, :, step] = both[:, sub, :, :, other].reshape(2 * own, -1)
            back_left[sub, :, step] = both[:, other, :, :, sub].reshape(2 * own, -1).T
    n_two = np.arange(COLS, dtype=np.int64)
    coarse = STEP * np.arange(big // STEP, dtype=np.int64)
    fine = np.arange(STEP, dtype=np.int64)
    angle = 2 * np.pi / (4 * length) * (4 * coarse[:, None] * n_two[None, :] % (4 * length))
    coarse = np.stack([np.cos(angle), -np.sin(angle)], 0).reshape(2, group, own // STEP, COLS)
    coarse = np.ascontiguousarray(coarse.transpose(1, 0, 2, 3))
    angle = 2 * np.pi / (4 * length) * ((4 * fine[:, None] + 1) * n_two[None, :] % (4 * length))
    fine = np.stack([np.cos(angle), -np.sin(angle)], 0)
    angle = 2 * np.pi / COLS * (n_two[:, None] * n_two[None, :] % COLS)
    return (
        left.reshape(group, 2 * own, big).astype(BF),
        back_left.reshape(group, chans * rows, 2 * big).astype(BF),
        np.concatenate([np.cos(angle), np.sin(angle)], 0).astype(BF),
        coarse.astype(np.float32),
        fine.astype(np.float32),
    )


def dot(left, right):
    return jnp.dot(left, right, preferred_element_type=F32)


def cost(flops):
    return pl.CostEstimate(flops=int(flops), bytes_accessed=0, transcendentals=0)


def params(mib):
    return pltpu.CompilerParams(vmem_limit_bytes=mib * 2**20)


def tables_kernel(group, *refs):
    left_hbm, back_hbm, wave_hbm, coarse_hbm, fine_hbm = refs[:5]
    left_ref, back_ref, wave_ref, turn_ref, coarse_ref, fine_ref, sems = refs[5:]
    sub = lax.rem(lax.axis_index("ctx"), group)
    copies = [
        pltpu.make_async_copy(coarse_hbm.at[sub], coarse_ref, sems.at[0]),
        pltpu.make_async_copy(fine_hbm, fine_ref, sems.at[1]),
        pltpu.make_async_copy(left_hbm.at[sub], left_ref, sems.at[2]),
        pltpu.make_async_copy(wave_hbm, wave_ref, sems.at[3]),
        pltpu.make_async_copy(back_hbm.at[sub], back_ref, sems.at[4]),
    ]
    for copy in copies:
        copy.start()
    copies[0].wait()
    copies[1].wait()
    fine_re, fine_im = fine_ref[0], fine_ref[1]
    for number in range(coarse_ref.shape[1]):
        tab_re = coarse_ref[0, number : number + 1]
        tab_im = coarse_ref[1, number : number + 1]
        cut = slice(number * STEP, (number + 1) * STEP)
        turn_ref[0, cut] = fine_re * tab_re - fine_im * tab_im
        turn_ref[1, cut] = fine_re * tab_im + fine_im * tab_re
    for copy in copies[2:]:
        copy.wait()


def run_tables(group, tables):
    left, back, wave, coarse, fine = tables
    own = left.shape[1] // 2
    return pl.pallas_call(
        functools.partial(tables_kernel, group),
        out_shape=(
            jax.ShapeDtypeStruct(left.shape[1:], BF),
            jax.ShapeDtypeStruct(back.shape[1:], BF),
            jax.ShapeDtypeStruct(wave.shape, BF),
            jax.ShapeDtypeStruct((2, own, COLS), F32),
        ),
        in_specs=[HBM] * 5,
        out_specs=(VMEM,) * 4,
        scratch_shapes=[
            pltpu.VMEM(coarse.shape[1:], F32),
            pltpu.VMEM(fine.shape, F32),
            pltpu.SemaphoreType.DMA((5,)),
        ],
        compiler_params=params(40),
        cost_estimate=cost(3e9),
        name="load_tables",
    )(*tables)


def spectrum_kernel(chans, group, scale, *refs):
    count = chans * group
    blocks, (left_ref, wave_ref, turn_ref, out_ref) = refs[:count], refs[count : count + 4]
    x_ref, mid_ref, prod_ref, spec_ref = refs[count + 4 :]
    rows = blocks[0].shape[1]
    own = mid_ref.shape[0]
    home = lax.axis_index("ctx") // group
    for step in range(group):
        for rel in range(chans):
            first = pl.multiple_of((step * chans + (home ^ rel)) * rows, rows)
            for kind in range(2):
                x_ref[kind, pl.ds(first, rows)] = blocks[step * chans + rel][kind]
    for kind in range(2):
        for tile in range(0, COLS, 256):
            cut = slice(tile, tile + 256)
            val = dot(left_ref[...], x_ref[kind, :, cut])
            val_re, val_im = val[:own], val[own:]
            tab_re, tab_im = turn_ref[0, :, cut], turn_ref[1, :, cut]
            mid_re = (val_re * tab_re - val_im * tab_im).astype(BF)
            mid_ref[:, cut] = mid_re
            mid_ref[:, COLS + tile : COLS + tile + 256] = (
                val_re * tab_im + val_im * tab_re
            ).astype(BF)
            mid_ref[:, 2 * COLS + tile : 2 * COLS + tile + 256] = -mid_re
        for tile in range(0, COLS, 256):
            cut = slice(tile, tile + 256)
            out_re = dot(mid_ref[:, : 2 * COLS], wave_ref[:, cut])
            out_im = dot(mid_ref[:, COLS:], wave_ref[:, cut])
            if kind == 0:
                spec_ref[0, :, cut] = out_re * scale
                spec_ref[1, :, cut] = out_im * scale
            else:
                fil_re, fil_im = spec_ref[0, :, cut], spec_ref[1, :, cut]
                prod_im = (out_re * fil_im + out_im * fil_re).astype(BF)
                prod_ref[:, cut] = prod_im
                prod_ref[:, COLS + tile : COLS + tile + 256] = (
                    out_re * fil_re - out_im * fil_im
                ).astype(BF)
                prod_ref[:, 2 * COLS + tile : 2 * COLS + tile + 256] = -prod_im
    for tile in range(0, COLS, 256):
        cut = slice(tile, tile + 256)
        val_im = dot(prod_ref[:, : 2 * COLS], wave_ref[:, cut])
        val_re = dot(prod_ref[:, COLS:], wave_ref[:, cut])
        tab_re, tab_im = turn_ref[0, :, cut], turn_ref[1, :, cut]
        out_ref[:own, cut] = (val_re * tab_re + val_im * tab_im).astype(BF)
        out_ref[own:, cut] = (val_im * tab_re - val_re * tab_im).astype(BF)


def position_kernel(chans, group, *refs):
    parts, table_ref = refs[:group], refs[group]
    outs, sum_ref = refs[group + 1 : group + 1 + chans], refs[group + 1 + chans]
    home = lax.axis_index("ctx") // group
    depth = parts[0].shape[0]
    total = dot(table_ref[:, :depth], parts[0][...])
    for step in range(1, group):
        total += dot(table_ref[:, step * depth : (step + 1) * depth], parts[step][...])
    sum_ref[...] = total.astype(BF)
    rows = outs[0].shape[0]
    for rel in range(chans):
        outs[rel][...] = sum_ref[pl.ds(pl.multiple_of((home ^ rel) * rows, rows), rows)]


def gate_kernel(chans, group, *refs):
    parts = refs[:chans]
    query_ref, key_ref, value_ref, gain_ref = refs[chans : chans + 4]
    outs = refs[chans + 4 :]
    home = lax.axis_index("ctx") // group
    for rel in range(chans):
        chan = home ^ rel
        signal = key_ref[chan].astype(F32) * value_ref[chan].astype(F32)
        total = parts[rel][...].astype(F32) + gain_ref[chan] * signal
        gated = (query_ref[chan].astype(F32) * total).astype(BF)
        for out, low, high in zip(outs, CUTS[:-1], CUTS[1:]):
            out[chan] = gated[:, low:high]


def run_spectrum(blocks, chans, group, tables, scale):
    left, _, wave, turn = tables
    own, big = left.shape[0] // 2, left.shape[1]
    return pl.pallas_call(
        functools.partial(spectrum_kernel, chans, group, scale),
        out_shape=jax.ShapeDtypeStruct((2 * own, COLS), BF),
        in_specs=[VMEM] * (len(blocks) + 3),
        out_specs=VMEM,
        scratch_shapes=[
            pltpu.VMEM((2, big, COLS), BF),
            pltpu.VMEM((own, 3 * COLS), BF),
            pltpu.VMEM((own, 3 * COLS), BF),
            pltpu.VMEM((2, own, COLS), F32),
        ],
        compiler_params=params(20),
        cost_estimate=cost(8 * own * COLS * (big + 3 * COLS)),
        name="spectrum_product",
    )(*blocks, left, wave, turn)


def run_position(parts, chans, group, table):
    out_rows, depth = table.shape
    rows = out_rows // chans
    return pl.pallas_call(
        functools.partial(position_kernel, chans, group),
        out_shape=(jax.ShapeDtypeStruct((rows, COLS), BF),) * chans,
        in_specs=[VMEM] * (group + 1),
        out_specs=(VMEM,) * chans,
        scratch_shapes=[pltpu.VMEM((out_rows, COLS), BF)],
        compiler_params=params(12),
        cost_estimate=cost(2 * out_rows * depth * COLS),
        name="back_positions",
    )(*parts, table)


def run_gate(parts, query, key, value, gain, group):
    chans, rows, _ = query.shape
    return pl.pallas_call(
        functools.partial(gate_kernel, chans, group),
        out_shape=tuple(
            jax.ShapeDtypeStruct((chans, rows, high - low), BF)
            for low, high in zip(CUTS[:-1], CUTS[1:])
        ),
        in_specs=[VMEM] * (chans + 3) + [SMEM],
        out_specs=(VMEM,) * (len(CUTS) - 1),
        compiler_params=params(12),
        cost_estimate=cost(4 * chans * rows * COLS),
        name="gate",
    )(*parts, query, key, value, gain)


def mix_kernel(chans, slots, outputs, plane_ref, weight_ref, *refs):
    count = len(slots)
    feats = refs[count].shape[0]

    @pl.loop(0, refs[0].shape[1] // 16)
    def _(index):
        rows = pl.ds(pl.multiple_of(index * 16, 16), 16)
        sums = [[None] * feats for _ in outputs]
        for slot, ref in zip(slots, refs[:count]):
            for chan in range(chans):
                value = ref[chan, rows].astype(F32)
                row = plane_ref[slot] * chans + chan
                for out, total in zip(outputs, sums):
                    for feat in range(feats):
                        term = value * weight_ref[row, plane_ref[out[0]] * feats + feat]
                        total[feat] = term if total[feat] is None else total[feat] + term
        for ref, total in zip(refs[count:], sums):
            for feat in range(feats):
                ref[feat, rows] = total[feat].astype(ref.dtype)


def run_mix(planes, weight, slots, outputs, values):
    chans, rows, cols = values[0].shape
    feats = weight.shape[1] // 4
    size = feats * rows * cols
    return pl.pallas_call(
        functools.partial(mix_kernel, chans, slots, outputs),
        out_shape=tuple(jax.ShapeDtypeStruct((feats, rows, cols), out[1]) for out in outputs),
        in_specs=[SMEM, SMEM] + [VMEM] * len(slots),
        out_specs=(VMEM,) * len(outputs),
        compiler_params=params(12),
        cost_estimate=cost(2 * chans * len(slots) * len(outputs) * size),
        name="mix_features",
    )(planes, weight, *values)


def line_mix(gated, out_weight):
    plane = lax.axis_index("tp")
    near = plane < 2
    planes = jnp.stack(
        [plane, jnp.where(near, 2, 1), jnp.where(near, 3, 0), jnp.where(near, 0, 3), plane ^ 1]
    ).astype(jnp.int32)
    own_at, mid_at, far_at, edge_at, pair_at = range(5)
    weight = out_weight.astype(F32)
    mix = functools.partial(run_mix, planes, weight)
    swapped, gathered = gated
    pair = lax.ppermute(swapped, "tp", [(0, 1), (1, 0), (2, 3), (3, 2)])
    far = lax.ppermute(gathered, "tp", [(0, 2), (3, 1)])
    mid = lax.ppermute(gathered, "tp", [(1, 2), (2, 1)])
    edge = lax.ppermute(gathered, "tp", [(0, 1), (3, 2)])
    to_mid, to_far = mix((own_at, pair_at), ((mid_at, BF), (far_at, BF)), (swapped, pair))
    from_far = lax.ppermute(to_far, "tp", [(1, 3), (2, 0)])
    from_mid = lax.ppermute(to_mid, "tp", [(1, 2), (2, 1)])
    far, mid, to_mid, to_far = lax.optimization_barrier((far, mid, to_mid, to_far))
    (to_edge,) = mix((own_at, far_at, mid_at), ((edge_at, BF),), (gathered, far, mid))
    from_edge = lax.ppermute(to_edge, "tp", [(2, 3), (1, 0)])
    (acc_swapped,) = mix((own_at, pair_at), ((own_at, F32),), (swapped, pair))
    (acc_gathered,) = mix(
        (own_at, far_at, mid_at, edge_at), ((own_at, F32),), (gathered, far, mid, edge)
    )
    done = (acc_swapped + from_far.astype(F32) + from_mid.astype(F32)).astype(BF)
    done, acc_gathered = lax.optimization_barrier((done, acc_gathered))
    return [done, (acc_gathered + from_edge.astype(F32)).astype(BF)]


def gather_mix(gated, out_weight):
    plane = lax.axis_index("tp")
    outs = out_weight.shape[1] // lax.axis_size("tp")
    own_cols = lax.dynamic_slice_in_dim(out_weight, plane * outs, outs, 1)
    return [
        jnp.einsum(
            "co,crl->orl",
            own_cols,
            lax.all_gather(own, "tp", axis=0, tiled=True),
            preferred_element_type=F32,
        ).astype(BF)
        for own in gated
    ]


def local(query_gate, key_branch, value_branch, long_filter, skip_gain, out_weight):
    ctx_count = lax.axis_size("ctx")
    chans, tok_count = query_gate.shape
    rows = tok_count // COLS
    group = ctx_count // chans
    length = ctx_count * tok_count
    home = lax.axis_index("ctx") // group
    shape = (chans, rows, COLS)
    tables = run_tables(group, make_tables(ctx_count, group, chans, rows))

    def swap(values):
        got = [values[0]]
        for rel in range(1, chans):
            pairs = [
                (group * chip + core, group * (chip ^ rel) + core)
                for chip in range(chans)
                for core in range(group)
            ]
            got.append(lax.ppermute(values[rel], "ctx", pairs))
        return got

    def shift(value, step):
        pairs = [
            (group * chip + core, group * chip + (core + step) % group)
            for chip in range(chans)
            for core in range(group)
        ]
        return lax.ppermute(value, "ctx", pairs)

    query = query_gate.reshape(shape)
    key = key_branch.reshape(shape)
    value = value_branch.reshape(shape)
    signal = (key.astype(F32) * value.astype(F32)).astype(BF)
    pairs = jnp.stack([long_filter.astype(BF).reshape(shape), signal], 1)
    blocks = [lax.dynamic_index_in_dim(pairs, home ^ rel, 0, False) for rel in range(chans)]
    blocks = swap(blocks)
    blocks, tables = lax.optimization_barrier((blocks, tables))
    blocks += [shift(part, -step) for step in range(1, group) for part in blocks]
    back = run_spectrum(blocks, chans, group, tables, 1.0 / length)
    parts = [back] + [shift(back, -step) for step in range(1, group)]
    parts = swap(list(run_position(parts, chans, group, tables[1])))
    gated = run_gate(parts, query, key, value, skip_gain, group)
    mixed = (line_mix if lax.axis_size("tp") == 4 else gather_mix)(gated, out_weight)
    return jnp.concatenate(mixed, 2).reshape(-1, tok_count)


def solution(mesh):
    placed = (P("tp", "ctx"), P("tp", "ctx"), P("tp", "ctx"), P("tp", "ctx"), P("tp"), P())
    return jax.shard_map(
        local, mesh=mesh, in_specs=placed, out_specs=P("tp", "ctx"), check_vma=False
    )
```

```python
import functools

import jax
import jax.numpy as jnp
import numpy as np
from jax import lax
from jax.experimental import pallas as pl
from jax.experimental.pallas import tpu as pltpu
from jax.sharding import PartitionSpec as P

COLS = 512
STEP = 32
PIECES = 4
CUTS = (0, 256, 512)
BF = jnp.bfloat16
F32 = jnp.float32
VMEM = pl.BlockSpec(memory_space=pltpu.VMEM)
SMEM = pl.BlockSpec(memory_space=pltpu.SMEM)
HBM = pl.BlockSpec(memory_space=pltpu.HBM)


def make_tables(ctx_count, group, chans, rows):
    big = ctx_count * rows
    own = big // group
    length = big * COLS
    k_one = np.arange(big, dtype=np.int64)
    n_one = np.arange(big, dtype=np.int64)
    angle = 2 * np.pi / (4 * big) * ((4 * k_one[:, None] + 1) * n_one[None, :] % (4 * big))
    both = np.stack([np.cos(angle), -np.sin(angle)], 0)
    both = both.reshape(2, group, own, chans, group, rows)
    left = np.empty((group, 2 * own, group, chans * rows))
    back_left = np.empty((group, chans * rows, group, 2 * own))
    for sub in range(group):
        for step in range(group):
            other = (sub + step) % group
            left[sub, :, step] = both[:, sub, :, :, other].reshape(2 * own, -1)
            back_left[sub, :, step] = both[:, other, :, :, sub].reshape(2 * own, -1).T
    n_two = np.arange(COLS, dtype=np.int64)
    coarse = STEP * np.arange(big // STEP, dtype=np.int64)
    fine = np.arange(STEP, dtype=np.int64)
    angle = 2 * np.pi / (4 * length) * (4 * coarse[:, None] * n_two[None, :] % (4 * length))
    coarse = np.stack([np.cos(angle), -np.sin(angle)], 0).reshape(2, group, own // STEP, COLS)
    coarse = np.ascontiguousarray(coarse.transpose(1, 0, 2, 3))
    angle = 2 * np.pi / (4 * length) * ((4 * fine[:, None] + 1) * n_two[None, :] % (4 * length))
    fine = np.stack([np.cos(angle), -np.sin(angle)], 0)
    angle = 2 * np.pi / COLS * (n_two[:, None] * n_two[None, :] % COLS)
    return (
        left.reshape(group, 2 * own, big).astype(BF),
        back_left.reshape(group, chans * rows, 2 * big).astype(BF),
        np.concatenate([np.cos(angle), np.sin(angle)], 0).astype(BF),
        coarse.astype(np.float32),
        fine.astype(np.float32),
    )


def dot(left, right):
    return jnp.dot(left, right, preferred_element_type=F32)


def cost(flops):
    return pl.CostEstimate(flops=int(flops), bytes_accessed=0, transcendentals=0)


def params(mib):
    return pltpu.CompilerParams(vmem_limit_bytes=mib * 2**20)


def tables_kernel(group, *refs):
    left_hbm, back_hbm, wave_hbm, coarse_hbm, fine_hbm = refs[:5]
    left_ref, back_ref, wave_ref, turn_ref, coarse_ref, fine_ref, sems = refs[5:]
    sub = lax.rem(lax.axis_index("ctx"), group)
    copies = [
        pltpu.make_async_copy(coarse_hbm.at[sub], coarse_ref, sems.at[0]),
        pltpu.make_async_copy(fine_hbm, fine_ref, sems.at[1]),
        pltpu.make_async_copy(left_hbm.at[sub], left_ref, sems.at[2]),
        pltpu.make_async_copy(wave_hbm, wave_ref, sems.at[3]),
        pltpu.make_async_copy(back_hbm.at[sub], back_ref, sems.at[4]),
    ]
    for copy in copies:
        copy.start()
    copies[0].wait()
    copies[1].wait()
    fine_re, fine_im = fine_ref[0], fine_ref[1]
    for number in range(coarse_ref.shape[1]):
        tab_re = coarse_ref[0, number : number + 1]
        tab_im = coarse_ref[1, number : number + 1]
        cut = slice(number * STEP, (number + 1) * STEP)
        turn_ref[0, cut] = fine_re * tab_re - fine_im * tab_im
        turn_ref[1, cut] = fine_re * tab_im + fine_im * tab_re
    for copy in copies[2:]:
        copy.wait()


def run_tables(group, tables):
    left, back, wave, coarse, fine = tables
    own = left.shape[1] // 2
    return pl.pallas_call(
        functools.partial(tables_kernel, group),
        out_shape=(
            jax.ShapeDtypeStruct(left.shape[1:], BF),
            jax.ShapeDtypeStruct(back.shape[1:], BF),
            jax.ShapeDtypeStruct(wave.shape, BF),
            jax.ShapeDtypeStruct((2, own, COLS), F32),
        ),
        in_specs=[HBM] * 5,
        out_specs=(VMEM,) * 4,
        scratch_shapes=[
            pltpu.VMEM(coarse.shape[1:], F32),
            pltpu.VMEM(fine.shape, F32),
            pltpu.SemaphoreType.DMA((5,)),
        ],
        compiler_params=params(40),
        cost_estimate=cost(3e9),
        name="load_tables",
    )(*tables)


def prepare_kernel(chans, group, *refs):
    filter_hbm, key_hbm, value_hbm = refs[:3]
    outs = refs[3 : 3 + chans]
    filter_ref, key_ref, value_ref, pair_ref, sems = refs[3 + chans :]
    home = lax.axis_index("ctx") // group
    rows = pair_ref.shape[2]
    step = rows // PIECES
    copies = []
    for number in range(PIECES):
        cut = slice(number * step * COLS, (number + 1) * step * COLS)
        for kind, (source, target) in enumerate(
            ((filter_hbm, filter_ref), (key_hbm, key_ref), (value_hbm, value_ref))
        ):
            copy = pltpu.make_async_copy(
                source.at[:, cut], target.at[:, cut], sems.at[kind, number]
            )
            copy.start()
            copies.append(copy)
    shape = (chans, 16, COLS)
    for number in range(PIECES):
        for copy in copies[3 * number : 3 * number + 3]:
            copy.wait()
        for first in range(number * step, (number + 1) * step, 16):
            cut = slice(first * COLS, (first + 16) * COLS)
            pair_ref[:, 0, first : first + 16] = filter_ref[:, cut].astype(BF).reshape(shape)
            signal = key_ref[:, cut].astype(F32) * value_ref[:, cut].astype(F32)
            pair_ref[:, 1, first : first + 16] = signal.astype(BF).reshape(shape)
    for rel in range(chans):
        outs[rel][...] = pair_ref[home ^ rel]


def run_prepare(long_filter, key, value, group):
    chans, tok_count = key.shape
    rows = tok_count // COLS
    return pl.pallas_call(
        functools.partial(prepare_kernel, chans, group),
        out_shape=(jax.ShapeDtypeStruct((2, rows, COLS), BF),) * chans,
        in_specs=[HBM] * 3,
        out_specs=(VMEM,) * chans,
        scratch_shapes=[
            pltpu.VMEM((chans, tok_count), F32),
            pltpu.VMEM((chans, tok_count), BF),
            pltpu.VMEM((chans, tok_count), BF),
            pltpu.VMEM((chans, 2, rows, COLS), BF),
            pltpu.SemaphoreType.DMA((3, PIECES)),
        ],
        compiler_params=params(60),
        cost_estimate=cost(4 * chans * tok_count),
        name="prepare_blocks",
    )(long_filter, key, value)


def finish_kernel(first_ref, acc_ref, got_ref, out_hbm, out_ref, sems):
    feats, rows, _ = first_ref.shape
    step = rows // PIECES
    copies = []
    for number in range(PIECES):
        for row in range(number * step, (number + 1) * step, 16):
            cut = slice(row, row + 16)
            second = (acc_ref[:, cut] + got_ref[:, cut].astype(F32)).astype(BF)
            whole = jnp.concatenate([first_ref[:, cut], second], 2)
            out_ref[:, row * COLS : (row + 16) * COLS] = whole.reshape(feats, 16 * COLS)
        cut = slice(number * step * COLS, (number + 1) * step * COLS)
        copy = pltpu.make_async_copy(out_ref.at[:, cut], out_hbm.at[:, cut], sems.at[number])
        copy.start()
        copies.append(copy)
    for copy in copies:
        copy.wait()


def run_finish(first, acc, got):
    feats, rows, _ = first.shape
    return pl.pallas_call(
        finish_kernel,
        out_shape=jax.ShapeDtypeStruct((feats, rows * COLS), BF),
        in_specs=[VMEM] * 3,
        out_specs=HBM,
        scratch_shapes=[
            pltpu.VMEM((feats, rows * COLS), BF),
            pltpu.SemaphoreType.DMA((PIECES,)),
        ],
        compiler_params=params(12),
        cost_estimate=cost(feats * rows * COLS),
        name="finish",
    )(first, acc, got)


def spectrum_kernel(chans, group, scale, *refs):
    count = chans * group
    blocks = refs[:count]
    left_ref, wave_ref, turn_ref, prod_ref, out_ref = refs[count : count + 5]
    x_ref, mid_ref, spec_ref = refs[count + 5 :]
    rows = blocks[0].shape[1]
    own = mid_ref.shape[0]
    home = lax.axis_index("ctx") // group
    for step in range(group):
        for rel in range(chans):
            first = pl.multiple_of((step * chans + (home ^ rel)) * rows, rows)
            for kind in range(2):
                x_ref[kind, pl.ds(first, rows)] = blocks[step * chans + rel][kind]
    for kind in range(2):
        for tile in range(0, COLS, 256):
            cut = slice(tile, tile + 256)
            val = dot(left_ref[...], x_ref[kind, :, cut])
            val_re, val_im = val[:own], val[own:]
            tab_re, tab_im = turn_ref[0, :, cut], turn_ref[1, :, cut]
            mid_re = (val_re * tab_re - val_im * tab_im).astype(BF)
            mid_ref[:, cut] = mid_re
            mid_ref[:, COLS + tile : COLS + tile + 256] = (
                val_re * tab_im + val_im * tab_re
            ).astype(BF)
            mid_ref[:, 2 * COLS + tile : 2 * COLS + tile + 256] = -mid_re
        for tile in range(0, COLS, 256):
            cut = slice(tile, tile + 256)
            out_re = dot(mid_ref[:, : 2 * COLS], wave_ref[:, cut])
            out_im = dot(mid_ref[:, COLS:], wave_ref[:, cut])
            if kind == 0:
                spec_ref[0, :, cut] = out_re * scale
                spec_ref[1, :, cut] = out_im * scale
            else:
                fil_re, fil_im = spec_ref[0, :, cut], spec_ref[1, :, cut]
                prod_im = (out_re * fil_im + out_im * fil_re).astype(BF)
                prod_ref[:, cut] = prod_im
                prod_ref[:, COLS + tile : COLS + tile + 256] = (
                    out_re * fil_re - out_im * fil_im
                ).astype(BF)
                prod_ref[:, 2 * COLS + tile : 2 * COLS + tile + 256] = -prod_im
    back_stage(CUTS[0], CUTS[1], prod_ref, wave_ref, turn_ref, out_ref)


def back_stage(low, high, prod_ref, wave_ref, turn_ref, out_ref):
    own = prod_ref.shape[0]
    cut = slice(low, high)
    val_im = dot(prod_ref[:, : 2 * COLS], wave_ref[:, cut])
    val_re = dot(prod_ref[:, COLS:], wave_ref[:, cut])
    tab_re, tab_im = turn_ref[0, :, cut], turn_ref[1, :, cut]
    out_ref[:own] = (val_re * tab_re + val_im * tab_im).astype(BF)
    out_ref[own:] = (val_im * tab_re - val_re * tab_im).astype(BF)


def position_kernel(chans, group, *refs):
    parts, table_ref = refs[:group], refs[group]
    outs, sum_ref = refs[group + 1 : group + 1 + chans], refs[group + 1 + chans]
    home = lax.axis_index("ctx") // group
    depth = parts[0].shape[0]
    total = dot(table_ref[:, :depth], parts[0][...])
    for step in range(1, group):
        total += dot(table_ref[:, step * depth : (step + 1) * depth], parts[step][...])
    sum_ref[...] = total.astype(BF)
    rows = outs[0].shape[0]
    for rel in range(chans):
        outs[rel][...] = sum_ref[pl.ds(pl.multiple_of((home ^ rel) * rows, rows), rows)]


def gate_kernel(chans, group, low, high, *refs):
    parts = refs[:chans]
    query_ref, key_ref, value_ref, gain_ref, out_ref = refs[chans:]
    cut = slice(low, high)
    home = lax.axis_index("ctx") // group
    for rel in range(chans):
        chan = home ^ rel
        signal = key_ref[chan, :, cut].astype(F32) * value_ref[chan, :, cut].astype(F32)
        total = parts[rel][...].astype(F32) + gain_ref[chan] * signal
        out_ref[chan] = (query_ref[chan, :, cut].astype(F32) * total).astype(BF)


def run_spectrum(blocks, chans, group, tables, scale):
    left, _, wave, turn = tables
    own, big = left.shape[0] // 2, left.shape[1]
    return pl.pallas_call(
        functools.partial(spectrum_kernel, chans, group, scale),
        out_shape=(
            jax.ShapeDtypeStruct((own, 3 * COLS), BF),
            jax.ShapeDtypeStruct((2 * own, CUTS[1] - CUTS[0]), BF),
        ),
        in_specs=[VMEM] * (len(blocks) + 3),
        out_specs=(VMEM, VMEM),
        scratch_shapes=[
            pltpu.VMEM((2, big, COLS), BF),
            pltpu.VMEM((own, 3 * COLS), BF),
            pltpu.VMEM((2, own, COLS), F32),
        ],
        compiler_params=params(20),
        cost_estimate=cost(8 * own * COLS * (big + 3 * COLS)),
        name="spectrum_product",
    )(*blocks, left, wave, turn)


def run_back(prod, tables, low, high):
    _, _, wave, turn = tables
    own = prod.shape[0]
    return pl.pallas_call(
        functools.partial(back_stage, low, high),
        out_shape=jax.ShapeDtypeStruct((2 * own, high - low), BF),
        in_specs=[VMEM] * 3,
        out_specs=VMEM,
        compiler_params=params(12),
        cost_estimate=cost(8 * own * COLS * (high - low)),
        name="back_columns",
    )(prod, wave, turn)


def run_position(parts, chans, group, table):
    out_rows, depth = table.shape
    cols = parts[0].shape[1]
    rows = out_rows // chans
    return pl.pallas_call(
        functools.partial(position_kernel, chans, group),
        out_shape=(jax.ShapeDtypeStruct((rows, cols), BF),) * chans,
        in_specs=[VMEM] * (group + 1),
        out_specs=(VMEM,) * chans,
        scratch_shapes=[pltpu.VMEM((out_rows, cols), BF)],
        compiler_params=params(12),
        cost_estimate=cost(2 * out_rows * depth * cols),
        name="back_positions",
    )(*parts, table)


def run_gate(parts, query, key, value, gain, group, low, high):
    chans, rows, _ = query.shape
    return pl.pallas_call(
        functools.partial(gate_kernel, chans, group, low, high),
        out_shape=jax.ShapeDtypeStruct((chans, rows, high - low), BF),
        in_specs=[VMEM] * (chans + 3) + [SMEM],
        out_specs=VMEM,
        compiler_params=params(12),
        cost_estimate=cost(4 * chans * rows * (high - low)),
        name="gate",
    )(*parts, query, key, value, gain)


def mix_kernel(chans, slots, outputs, plane_ref, weight_ref, *refs):
    count = len(slots)
    feats = refs[count].shape[0]

    @pl.loop(0, refs[0].shape[1] // 16)
    def _(index):
        rows = pl.ds(pl.multiple_of(index * 16, 16), 16)
        sums = [[None] * feats for _ in outputs]
        for slot, ref in zip(slots, refs[:count]):
            for chan in range(chans):
                value = ref[chan, rows].astype(F32)
                row = plane_ref[slot] * chans + chan
                for out, total in zip(outputs, sums):
                    for feat in range(feats):
                        term = value * weight_ref[row, plane_ref[out[0]] * feats + feat]
                        total[feat] = term if total[feat] is None else total[feat] + term
        for ref, total in zip(refs[count:], sums):
            for feat in range(feats):
                ref[feat, rows] = total[feat].astype(ref.dtype)


def run_mix(planes, weight, slots, outputs, values):
    chans, rows, cols = values[0].shape
    feats = weight.shape[1] // 4
    size = feats * rows * cols
    return pl.pallas_call(
        functools.partial(mix_kernel, chans, slots, outputs),
        out_shape=tuple(jax.ShapeDtypeStruct((feats, rows, cols), out[1]) for out in outputs),
        in_specs=[SMEM, SMEM] + [VMEM] * len(slots),
        out_specs=(VMEM,) * len(outputs),
        compiler_params=params(12),
        cost_estimate=cost(2 * chans * len(slots) * len(outputs) * size),
        name="mix_features",
    )(planes, weight, *values)


def line_mix(gated, out_weight):
    plane = lax.axis_index("tp")
    near = plane < 2
    planes = jnp.stack(
        [plane, jnp.where(near, 2, 1), jnp.where(near, 3, 0), jnp.where(near, 0, 3), plane ^ 1]
    ).astype(jnp.int32)
    own_at, mid_at, far_at, edge_at, pair_at = range(5)
    weight = out_weight.astype(F32)
    mix = functools.partial(run_mix, planes, weight)
    swapped, gathered = gated
    far = lax.ppermute(gathered, "tp", [(0, 2), (3, 1)])
    mid = lax.ppermute(gathered, "tp", [(1, 2), (2, 1)])
    pair = lax.ppermute(swapped, "tp", [(0, 1), (1, 0), (2, 3), (3, 2)])
    to_mid, to_far = mix((own_at, pair_at), ((mid_at, BF), (far_at, BF)), (swapped, pair))
    from_far = lax.ppermute(to_far, "tp", [(1, 3), (2, 0)])
    from_mid = lax.ppermute(to_mid, "tp", [(1, 2), (2, 1)])
    gathered, _ = lax.optimization_barrier((gathered, to_mid))
    edge = lax.ppermute(gathered, "tp", [(0, 1), (3, 2)])
    far, mid, to_mid, to_far = lax.optimization_barrier((far, mid, to_mid, to_far))
    (to_edge,) = mix((own_at, far_at, mid_at), ((edge_at, BF),), (gathered, far, mid))
    from_edge = lax.ppermute(to_edge, "tp", [(2, 3), (1, 0)])
    (acc_swapped,) = mix((own_at, pair_at), ((own_at, F32),), (swapped, pair))
    (acc_gathered,) = mix(
        (own_at, far_at, mid_at, edge_at), ((own_at, F32),), (gathered, far, mid, edge)
    )
    done = (acc_swapped + from_far.astype(F32) + from_mid.astype(F32)).astype(BF)
    done, acc_gathered = lax.optimization_barrier((done, acc_gathered))
    return run_finish(done, acc_gathered, from_edge)


def gather_mix(gated, out_weight):
    plane = lax.axis_index("tp")
    outs = out_weight.shape[1] // lax.axis_size("tp")
    own_cols = lax.dynamic_slice_in_dim(out_weight, plane * outs, outs, 1)
    mixed = [
        jnp.einsum(
            "co,crl->orl",
            own_cols,
            lax.all_gather(own, "tp", axis=0, tiled=True),
            preferred_element_type=F32,
        ).astype(BF)
        for own in gated
    ]
    return jnp.concatenate(mixed, 2).reshape(outs, -1)


def local(query_gate, key_branch, value_branch, long_filter, skip_gain, out_weight):
    ctx_count = lax.axis_size("ctx")
    chans, tok_count = query_gate.shape
    rows = tok_count // COLS
    group = ctx_count // chans
    length = ctx_count * tok_count
    shape = (chans, rows, COLS)
    tables = run_tables(group, make_tables(ctx_count, group, chans, rows))

    def swap(values):
        got = [values[0]]
        for rel in range(1, chans):
            pairs = [
                (group * chip + core, group * (chip ^ rel) + core)
                for chip in range(chans)
                for core in range(group)
            ]
            got.append(lax.ppermute(values[rel], "ctx", pairs))
        return got

    def shift(value, step):
        pairs = [
            (group * chip + core, group * chip + (core + step) % group)
            for chip in range(chans)
            for core in range(group)
        ]
        return lax.ppermute(value, "ctx", pairs)

    query = query_gate.reshape(shape)
    key = key_branch.reshape(shape)
    value = value_branch.reshape(shape)
    blocks = run_prepare(long_filter, key_branch, value_branch, group)
    blocks = swap(list(blocks))
    blocks, tables = lax.optimization_barrier((blocks, tables))
    blocks += [shift(part, -step) for step in range(1, group) for part in blocks]
    spans = list(zip(CUTS[:-1], CUTS[1:]))
    prod, back = run_spectrum(blocks, chans, group, tables, 1.0 / length)
    backs = [back] + [run_back(prod, tables, *span) for span in spans[1:]]
    places = []
    for back in backs:
        parts = [back] + [shift(back, -step) for step in range(1, group)]
        places.append(run_position(parts, chans, group, tables[1]))
    gated = []
    parts = swap(list(places[0]))
    for number, span in enumerate(spans):
        if number + 1 < len(spans):
            parts, _ = lax.optimization_barrier((parts, places[number + 1]))
        if number > 0:
            parts, gated[-1] = lax.optimization_barrier((parts, gated[-1]))
        gated.append(run_gate(parts, query, key, value, skip_gain, group, *span))
        if number + 1 < len(spans):
            parts = swap(list(places[number + 1]))
    return (line_mix if lax.axis_size("tp") == 4 else gather_mix)(gated, out_weight)


def solution(mesh):
    placed = (P("tp", "ctx"), P("tp", "ctx"), P("tp", "ctx"), P("tp", "ctx"), P("tp"), P())
    return jax.shard_map(
        local, mesh=mesh, in_specs=placed, out_specs=P("tp", "ctx"), check_vma=False
    )
```

```python
import functools

import jax
import jax.numpy as jnp
import numpy as np
from jax import lax
from jax.experimental import pallas as pl
from jax.experimental.pallas import tpu as pltpu
from jax.sharding import PartitionSpec as P

COLS = 512
STEP = 32
PIECES = 4
CUTS = (0, 256, 512)
BF = jnp.bfloat16
F32 = jnp.float32
VMEM = pl.BlockSpec(memory_space=pltpu.VMEM)
SMEM = pl.BlockSpec(memory_space=pltpu.SMEM)
HBM = pl.BlockSpec(memory_space=pltpu.HBM)


def make_tables(ctx_count, group, chans, rows):
    big = ctx_count * rows
    own = big // group
    length = big * COLS
    k_one = np.arange(big, dtype=np.int64)
    n_one = np.arange(big, dtype=np.int64)
    angle = 2 * np.pi / (4 * big) * ((4 * k_one[:, None] + 1) * n_one[None, :] % (4 * big))
    both = np.stack([np.cos(angle), -np.sin(angle)], 0)
    both = both.reshape(2, group, own, chans, group, rows)
    left = np.empty((group, 2 * own, group, chans * rows))
    back_left = np.empty((group, chans * rows, group, 2 * own))
    for sub in range(group):
        for step in range(group):
            other = (sub + step) % group
            left[sub, :, step] = both[:, sub, :, :, other].reshape(2 * own, -1)
            back_left[sub, :, step] = both[:, other, :, :, sub].reshape(2 * own, -1).T
    n_two = np.arange(COLS, dtype=np.int64)
    coarse = STEP * np.arange(big // STEP, dtype=np.int64)
    fine = np.arange(STEP, dtype=np.int64)
    angle = 2 * np.pi / (4 * length) * (4 * coarse[:, None] * n_two[None, :] % (4 * length))
    coarse = np.stack([np.cos(angle), -np.sin(angle)], 0).reshape(2, group, own // STEP, COLS)
    coarse = np.ascontiguousarray(coarse.transpose(1, 0, 2, 3))
    angle = 2 * np.pi / (4 * length) * ((4 * fine[:, None] + 1) * n_two[None, :] % (4 * length))
    fine = np.stack([np.cos(angle), -np.sin(angle)], 0)
    angle = 2 * np.pi / COLS * (n_two[:, None] * n_two[None, :] % COLS)
    return (
        left.reshape(group, 2 * own, big).astype(BF),
        back_left.reshape(group, chans * rows, 2 * big).astype(BF),
        np.concatenate([np.cos(angle), np.sin(angle)], 0).astype(BF),
        coarse.astype(np.float32),
        fine.astype(np.float32),
    )


def dot(left, right):
    return jnp.dot(left, right, preferred_element_type=F32)


def cost(flops):
    return pl.CostEstimate(flops=int(flops), bytes_accessed=0, transcendentals=0)


def params(mib):
    return pltpu.CompilerParams(vmem_limit_bytes=mib * 2**20)


def tables_kernel(group, *refs):
    left_hbm, back_hbm, wave_hbm, coarse_hbm, fine_hbm = refs[:5]
    left_ref, back_ref, wave_ref, turn_ref, coarse_ref, fine_ref, sems = refs[5:]
    sub = lax.rem(lax.axis_index("ctx"), group)
    copies = [
        pltpu.make_async_copy(coarse_hbm.at[sub], coarse_ref, sems.at[0]),
        pltpu.make_async_copy(fine_hbm, fine_ref, sems.at[1]),
        pltpu.make_async_copy(left_hbm.at[sub], left_ref, sems.at[2]),
        pltpu.make_async_copy(wave_hbm, wave_ref, sems.at[3]),
        pltpu.make_async_copy(back_hbm.at[sub], back_ref, sems.at[4]),
    ]
    for copy in copies:
        copy.start()
    copies[0].wait()
    copies[1].wait()
    fine_re, fine_im = fine_ref[0], fine_ref[1]
    for number in range(coarse_ref.shape[1]):
        tab_re = coarse_ref[0, number : number + 1]
        tab_im = coarse_ref[1, number : number + 1]
        cut = slice(number * STEP, (number + 1) * STEP)
        turn_ref[0, cut] = fine_re * tab_re - fine_im * tab_im
        turn_ref[1, cut] = fine_re * tab_im + fine_im * tab_re
    for copy in copies[2:]:
        copy.wait()


def run_tables(group, tables):
    left, back, wave, coarse, fine = tables
    own = left.shape[1] // 2
    return pl.pallas_call(
        functools.partial(tables_kernel, group),
        out_shape=(
            jax.ShapeDtypeStruct(left.shape[1:], BF),
            jax.ShapeDtypeStruct(back.shape[1:], BF),
            jax.ShapeDtypeStruct(wave.shape, BF),
            jax.ShapeDtypeStruct((2, own, COLS), F32),
        ),
        in_specs=[HBM] * 5,
        out_specs=(VMEM,) * 4,
        scratch_shapes=[
            pltpu.VMEM(coarse.shape[1:], F32),
            pltpu.VMEM(fine.shape, F32),
            pltpu.SemaphoreType.DMA((5,)),
        ],
        compiler_params=params(40),
        cost_estimate=cost(3e9),
        name="load_tables",
    )(*tables)


def prepare_kernel(chans, group, *refs):
    filter_hbm, key_hbm, value_hbm = refs[:3]
    outs = refs[3 : 3 + chans]
    filter_ref, key_ref, value_ref, pair_ref, sems = refs[3 + chans :]
    home = lax.axis_index("ctx") // group
    rows = pair_ref.shape[2]
    step = rows // PIECES
    copies = []
    for number in range(PIECES):
        cut = slice(number * step * COLS, (number + 1) * step * COLS)
        for kind, (source, target) in enumerate(
            ((filter_hbm, filter_ref), (key_hbm, key_ref), (value_hbm, value_ref))
        ):
            copy = pltpu.make_async_copy(
                source.at[:, cut], target.at[:, cut], sems.at[kind, number]
            )
            copy.start()
            copies.append(copy)
    shape = (chans, 16, COLS)
    for number in range(PIECES):
        for copy in copies[3 * number : 3 * number + 3]:
            copy.wait()
        for first in range(number * step, (number + 1) * step, 16):
            cut = slice(first * COLS, (first + 16) * COLS)
            pair_ref[:, 0, first : first + 16] = filter_ref[:, cut].astype(BF).reshape(shape)
            signal = key_ref[:, cut].astype(F32) * value_ref[:, cut].astype(F32)
            pair_ref[:, 1, first : first + 16] = signal.astype(BF).reshape(shape)
    for rel in range(chans):
        outs[rel][...] = pair_ref[home ^ rel]


def run_prepare(long_filter, key, value, group):
    chans, tok_count = key.shape
    rows = tok_count // COLS
    return pl.pallas_call(
        functools.partial(prepare_kernel, chans, group),
        out_shape=(jax.ShapeDtypeStruct((2, rows, COLS), BF),) * chans,
        in_specs=[HBM] * 3,
        out_specs=(VMEM,) * chans,
        scratch_shapes=[
            pltpu.VMEM((chans, tok_count), F32),
            pltpu.VMEM((chans, tok_count), BF),
            pltpu.VMEM((chans, tok_count), BF),
            pltpu.VMEM((chans, 2, rows, COLS), BF),
            pltpu.SemaphoreType.DMA((3, PIECES)),
        ],
        compiler_params=params(60),
        cost_estimate=cost(4 * chans * tok_count),
        name="prepare_blocks",
    )(long_filter, key, value)


def finish_kernel(first_ref, acc_ref, got_ref, out_hbm, out_ref, sems):
    feats, rows, _ = first_ref.shape
    step = rows // PIECES
    copies = []
    for number in range(PIECES):
        for row in range(number * step, (number + 1) * step, 16):
            cut = slice(row, row + 16)
            second = (acc_ref[:, cut] + got_ref[:, cut].astype(F32)).astype(BF)
            whole = jnp.concatenate([first_ref[:, cut], second], 2)
            out_ref[:, row * COLS : (row + 16) * COLS] = whole.reshape(feats, 16 * COLS)
        cut = slice(number * step * COLS, (number + 1) * step * COLS)
        copy = pltpu.make_async_copy(out_ref.at[:, cut], out_hbm.at[:, cut], sems.at[number])
        copy.start()
        copies.append(copy)
    for copy in copies:
        copy.wait()


def run_finish(first, acc, got):
    feats, rows, _ = first.shape
    return pl.pallas_call(
        finish_kernel,
        out_shape=jax.ShapeDtypeStruct((feats, rows * COLS), BF),
        in_specs=[VMEM] * 3,
        out_specs=HBM,
        scratch_shapes=[
            pltpu.VMEM((feats, rows * COLS), BF),
            pltpu.SemaphoreType.DMA((PIECES,)),
        ],
        compiler_params=params(12),
        cost_estimate=cost(feats * rows * COLS),
        name="finish",
    )(first, acc, got)


def spectrum_kernel(chans, group, scale, *refs):
    count = chans * group
    blocks = refs[:count]
    left_ref, wave_ref, turn_ref, prod_ref, out_ref = refs[count : count + 5]
    x_ref, mid_ref, spec_ref = refs[count + 5 :]
    rows = blocks[0].shape[1]
    own = mid_ref.shape[0]
    home = lax.axis_index("ctx") // group
    for step in range(group):
        for rel in range(chans):
            first = pl.multiple_of((step * chans + (home ^ rel)) * rows, rows)
            for kind in range(2):
                x_ref[kind, pl.ds(first, rows)] = blocks[step * chans + rel][kind]
    for kind in range(2):
        for tile in range(0, COLS, 256):
            cut = slice(tile, tile + 256)
            val = dot(left_ref[...], x_ref[kind, :, cut])
            val_re, val_im = val[:own], val[own:]
            tab_re, tab_im = turn_ref[0, :, cut], turn_ref[1, :, cut]
            mid_re = (val_re * tab_re - val_im * tab_im).astype(BF)
            mid_ref[:, cut] = mid_re
            mid_ref[:, COLS + tile : COLS + tile + 256] = (
                val_re * tab_im + val_im * tab_re
            ).astype(BF)
            mid_ref[:, 2 * COLS + tile : 2 * COLS + tile + 256] = -mid_re
        for tile in range(0, COLS, 256):
            cut = slice(tile, tile + 256)
            out_re = dot(mid_ref[:, : 2 * COLS], wave_ref[:, cut])
            out_im = dot(mid_ref[:, COLS:], wave_ref[:, cut])
            if kind == 0:
                spec_ref[0, :, cut] = out_re * scale
                spec_ref[1, :, cut] = out_im * scale
            else:
                fil_re, fil_im = spec_ref[0, :, cut], spec_ref[1, :, cut]
                prod_im = (out_re * fil_im + out_im * fil_re).astype(BF)
                prod_ref[:, cut] = prod_im
                prod_ref[:, COLS + tile : COLS + tile + 256] = (
                    out_re * fil_re - out_im * fil_im
                ).astype(BF)
                prod_ref[:, 2 * COLS + tile : 2 * COLS + tile + 256] = -prod_im
    back_stage(CUTS[0], CUTS[1], prod_ref, wave_ref, turn_ref, out_ref)


def back_stage(low, high, prod_ref, wave_ref, turn_ref, out_ref):
    own = prod_ref.shape[0]
    cut = slice(low, high)
    val_im = dot(prod_ref[:, : 2 * COLS], wave_ref[:, cut])
    val_re = dot(prod_ref[:, COLS:], wave_ref[:, cut])
    tab_re, tab_im = turn_ref[0, :, cut], turn_ref[1, :, cut]
    out_ref[:own] = (val_re * tab_re + val_im * tab_im).astype(BF)
    out_ref[own:] = (val_im * tab_re - val_re * tab_im).astype(BF)


def position_kernel(chans, group, *refs):
    parts, table_ref = refs[:group], refs[group]
    outs, sum_ref = refs[group + 1 : group + 1 + chans], refs[group + 1 + chans]
    home = lax.axis_index("ctx") // group
    depth = parts[0].shape[0]
    total = dot(table_ref[:, :depth], parts[0][...])
    for step in range(1, group):
        total += dot(table_ref[:, step * depth : (step + 1) * depth], parts[step][...])
    sum_ref[...] = total.astype(BF)
    rows = outs[0].shape[0]
    for rel in range(chans):
        outs[rel][...] = sum_ref[pl.ds(pl.multiple_of((home ^ rel) * rows, rows), rows)]


def gate_kernel(chans, group, low, high, *refs):
    parts = refs[:chans]
    query_ref, key_ref, value_ref, gain_ref, out_ref = refs[chans:]
    cut = slice(low, high)
    home = lax.axis_index("ctx") // group
    for rel in range(chans):
        chan = home ^ rel
        signal = key_ref[chan, :, cut].astype(F32) * value_ref[chan, :, cut].astype(F32)
        total = parts[rel][...].astype(F32) + gain_ref[chan] * signal
        out_ref[chan] = (query_ref[chan, :, cut].astype(F32) * total).astype(BF)


def run_spectrum(blocks, chans, group, tables, scale):
    left, _, wave, turn = tables
    own, big = left.shape[0] // 2, left.shape[1]
    return pl.pallas_call(
        functools.partial(spectrum_kernel, chans, group, scale),
        out_shape=(
            jax.ShapeDtypeStruct((own, 3 * COLS), BF),
            jax.ShapeDtypeStruct((2 * own, CUTS[1] - CUTS[0]), BF),
        ),
        in_specs=[VMEM] * (len(blocks) + 3),
        out_specs=(VMEM, VMEM),
        scratch_shapes=[
            pltpu.VMEM((2, big, COLS), BF),
            pltpu.VMEM((own, 3 * COLS), BF),
            pltpu.VMEM((2, own, COLS), F32),
        ],
        compiler_params=params(20),
        cost_estimate=cost(8 * own * COLS * (big + 3 * COLS)),
        name="spectrum_product",
    )(*blocks, left, wave, turn)


def run_back(prod, tables, low, high):
    _, _, wave, turn = tables
    own = prod.shape[0]
    return pl.pallas_call(
        functools.partial(back_stage, low, high),
        out_shape=jax.ShapeDtypeStruct((2 * own, high - low), BF),
        in_specs=[VMEM] * 3,
        out_specs=VMEM,
        compiler_params=params(12),
        cost_estimate=cost(8 * own * COLS * (high - low)),
        name="back_columns",
    )(prod, wave, turn)


def run_position(parts, chans, group, table):
    out_rows, depth = table.shape
    cols = parts[0].shape[1]
    rows = out_rows // chans
    return pl.pallas_call(
        functools.partial(position_kernel, chans, group),
        out_shape=(jax.ShapeDtypeStruct((rows, cols), BF),) * chans,
        in_specs=[VMEM] * (group + 1),
        out_specs=(VMEM,) * chans,
        scratch_shapes=[pltpu.VMEM((out_rows, cols), BF)],
        compiler_params=params(12),
        cost_estimate=cost(2 * out_rows * depth * cols),
        name="back_positions",
    )(*parts, table)


def run_gate(parts, query, key, value, gain, group, low, high):
    chans, rows, _ = query.shape
    return pl.pallas_call(
        functools.partial(gate_kernel, chans, group, low, high),
        out_shape=jax.ShapeDtypeStruct((chans, rows, high - low), BF),
        in_specs=[VMEM] * (chans + 3) + [SMEM],
        out_specs=VMEM,
        compiler_params=params(12),
        cost_estimate=cost(4 * chans * rows * (high - low)),
        name="gate",
    )(*parts, query, key, value, gain)


def mix_kernel(chans, slots, outputs, plane_ref, weight_ref, *refs):
    count = len(slots)
    feats = refs[count].shape[0]

    @pl.loop(0, refs[0].shape[1] // 16)
    def _(index):
        rows = pl.ds(pl.multiple_of(index * 16, 16), 16)
        sums = [[None] * feats for _ in outputs]
        for slot, ref in zip(slots, refs[:count]):
            for chan in range(chans):
                value = ref[chan, rows].astype(F32)
                row = plane_ref[slot] * chans + chan
                for out, total in zip(outputs, sums):
                    for feat in range(feats):
                        term = value * weight_ref[row, plane_ref[out[0]] * feats + feat]
                        total[feat] = term if total[feat] is None else total[feat] + term
        for ref, total in zip(refs[count:], sums):
            for feat in range(feats):
                ref[feat, rows] = total[feat].astype(ref.dtype)


def run_mix(planes, weight, slots, outputs, values):
    chans, rows, cols = values[0].shape
    feats = weight.shape[1] // 4
    size = feats * rows * cols
    return pl.pallas_call(
        functools.partial(mix_kernel, chans, slots, outputs),
        out_shape=tuple(jax.ShapeDtypeStruct((feats, rows, cols), out[1]) for out in outputs),
        in_specs=[SMEM, SMEM] + [VMEM] * len(slots),
        out_specs=(VMEM,) * len(outputs),
        compiler_params=params(12),
        cost_estimate=cost(2 * chans * len(slots) * len(outputs) * size),
        name="mix_features",
    )(planes, weight, *values)


def line_mix(gated, out_weight):
    plane = lax.axis_index("tp")
    near = plane < 2
    planes = jnp.stack(
        [plane, jnp.where(near, 2, 1), jnp.where(near, 3, 0), jnp.where(near, 0, 3), plane ^ 1]
    ).astype(jnp.int32)
    own_at, mid_at, far_at, edge_at, pair_at = range(5)
    weight = out_weight.astype(F32)
    mix = functools.partial(run_mix, planes, weight)
    swapped, gathered = gated
    far = lax.ppermute(gathered, "tp", [(0, 2), (3, 1)])
    mid = lax.ppermute(gathered, "tp", [(1, 2), (2, 1)])
    pair = lax.ppermute(swapped, "tp", [(0, 1), (1, 0), (2, 3), (3, 2)])
    to_mid, to_far = mix((own_at, pair_at), ((mid_at, BF), (far_at, BF)), (swapped, pair))
    from_far = lax.ppermute(to_far, "tp", [(1, 3), (2, 0)])
    from_mid = lax.ppermute(to_mid, "tp", [(1, 2), (2, 1)])
    gathered, _ = lax.optimization_barrier((gathered, to_mid))
    edge = lax.ppermute(gathered, "tp", [(0, 1), (3, 2)])
    far, mid, to_mid, to_far = lax.optimization_barrier((far, mid, to_mid, to_far))
    (to_edge,) = mix((own_at, far_at, mid_at), ((edge_at, BF),), (gathered, far, mid))
    from_edge = lax.ppermute(to_edge, "tp", [(2, 3), (1, 0)])
    (acc_swapped,) = mix((own_at, pair_at), ((own_at, F32),), (swapped, pair))
    (acc_gathered,) = mix(
        (own_at, far_at, mid_at, edge_at), ((own_at, F32),), (gathered, far, mid, edge)
    )
    done = (acc_swapped + from_far.astype(F32) + from_mid.astype(F32)).astype(BF)
    done, acc_gathered = lax.optimization_barrier((done, acc_gathered))
    return run_finish(done, acc_gathered, from_edge)


def gather_mix(gated, out_weight):
    plane = lax.axis_index("tp")
    outs = out_weight.shape[1] // lax.axis_size("tp")
    own_cols = lax.dynamic_slice_in_dim(out_weight, plane * outs, outs, 1)
    mixed = [
        jnp.einsum(
            "co,crl->orl",
            own_cols,
            lax.all_gather(own, "tp", axis=0, tiled=True),
            preferred_element_type=F32,
        ).astype(BF)
        for own in gated
    ]
    return jnp.concatenate(mixed, 2).reshape(outs, -1)


def local(query_gate, key_branch, value_branch, long_filter, skip_gain, out_weight):
    ctx_count = lax.axis_size("ctx")
    chans, tok_count = query_gate.shape
    rows = tok_count // COLS
    group = ctx_count // chans
    length = ctx_count * tok_count
    shape = (chans, rows, COLS)
    tables = run_tables(group, make_tables(ctx_count, group, chans, rows))

    def swap(values):
        got = [values[0]]
        for rel in range(1, chans):
            pairs = [
                (group * chip + core, group * (chip ^ rel) + core)
                for chip in range(chans)
                for core in range(group)
            ]
            got.append(lax.ppermute(values[rel], "ctx", pairs))
        return got

    def shift(value, step):
        pairs = [
            (group * chip + core, group * chip + (core + step) % group)
            for chip in range(chans)
            for core in range(group)
        ]
        return lax.ppermute(value, "ctx", pairs)

    query = query_gate.reshape(shape)
    key = key_branch.reshape(shape)
    value = value_branch.reshape(shape)
    blocks = run_prepare(long_filter, key_branch, value_branch, group)
    blocks = swap(list(blocks))
    blocks[-1], tables = lax.optimization_barrier((blocks[-1], tables))
    blocks += [shift(part, -step) for step in range(1, group) for part in blocks]
    spans = list(zip(CUTS[:-1], CUTS[1:]))
    prod, back = run_spectrum(blocks, chans, group, tables, 1.0 / length)
    backs = [back] + [run_back(prod, tables, *span) for span in spans[1:]]
    places = []
    for back in backs:
        parts = [back] + [shift(back, -step) for step in range(1, group)]
        places.append(run_position(parts, chans, group, tables[1]))
    gated = []
    parts = swap(list(places[0]))
    for number, span in enumerate(spans):
        if number + 1 < len(spans):
            parts, _ = lax.optimization_barrier((parts, places[number + 1]))
        if number > 0:
            parts, gated[-1] = lax.optimization_barrier((parts, gated[-1]))
        gated.append(run_gate(parts, query, key, value, skip_gain, group, *span))
        if number + 1 < len(spans):
            parts = swap(list(places[number + 1]))
    return (line_mix if lax.axis_size("tp") == 4 else gather_mix)(gated, out_weight)


def solution(mesh):
    placed = (P("tp", "ctx"), P("tp", "ctx"), P("tp", "ctx"), P("tp", "ctx"), P("tp"), P())
    return jax.shard_map(
        local, mesh=mesh, in_specs=placed, out_specs=P("tp", "ctx"), check_vma=False
    )
```

```python
import functools

import jax
import jax.numpy as jnp
import numpy as np
from jax import lax
from jax.experimental import pallas as pl
from jax.experimental.pallas import tpu as pltpu
from jax.sharding import PartitionSpec as P

COLS = 512
STEP = 32
PIECES = 4
CUTS = (0, 256, 512)
BF = jnp.bfloat16
F32 = jnp.float32
VMEM = pl.BlockSpec(memory_space=pltpu.VMEM)
SMEM = pl.BlockSpec(memory_space=pltpu.SMEM)
HBM = pl.BlockSpec(memory_space=pltpu.HBM)


def make_tables(ctx_count, group, chans, rows):
    big = ctx_count * rows
    own = big // group
    length = big * COLS
    k_one = np.arange(big, dtype=np.int64)
    n_one = np.arange(big, dtype=np.int64)
    angle = 2 * np.pi / (4 * big) * ((4 * k_one[:, None] + 1) * n_one[None, :] % (4 * big))
    both = np.stack([np.cos(angle), -np.sin(angle)], 0)
    both = both.reshape(2, group, own, chans, group, rows)
    left = np.empty((group, 2 * own, group, chans * rows))
    back_left = np.empty((group, chans * rows, group, 2 * own))
    for sub in range(group):
        for step in range(group):
            other = (sub + step) % group
            left[sub, :, step] = both[:, sub, :, :, other].reshape(2 * own, -1)
            back_left[sub, :, step] = both[:, other, :, :, sub].reshape(2 * own, -1).T
    n_two = np.arange(COLS, dtype=np.int64)
    coarse = STEP * np.arange(big // STEP, dtype=np.int64)
    fine = np.arange(STEP, dtype=np.int64)
    angle = 2 * np.pi / (4 * length) * (4 * coarse[:, None] * n_two[None, :] % (4 * length))
    coarse = np.stack([np.cos(angle), -np.sin(angle)], 0).reshape(2, group, own // STEP, COLS)
    coarse = np.ascontiguousarray(coarse.transpose(1, 0, 2, 3))
    angle = 2 * np.pi / (4 * length) * ((4 * fine[:, None] + 1) * n_two[None, :] % (4 * length))
    fine = np.stack([np.cos(angle), -np.sin(angle)], 0)
    angle = 2 * np.pi / COLS * (n_two[:, None] * n_two[None, :] % COLS)
    return (
        left.reshape(group, 2 * own, big).astype(BF),
        back_left.reshape(group, chans * rows, 2 * big).astype(BF),
        np.concatenate([np.cos(angle), np.sin(angle)], 0).astype(BF),
        coarse.astype(np.float32),
        fine.astype(np.float32),
    )


def dot(left, right):
    return jnp.dot(left, right, preferred_element_type=F32)


def cost(flops):
    return pl.CostEstimate(flops=int(flops), bytes_accessed=0, transcendentals=0)


def params(mib):
    return pltpu.CompilerParams(vmem_limit_bytes=mib * 2**20)


def tables_kernel(group, *refs):
    left_hbm, back_hbm, wave_hbm, coarse_hbm, fine_hbm = refs[:5]
    left_ref, back_ref, wave_ref, turn_ref, coarse_ref, fine_ref, sems = refs[5:]
    sub = lax.rem(lax.axis_index("ctx"), group)
    copies = [
        pltpu.make_async_copy(coarse_hbm.at[sub], coarse_ref, sems.at[0]),
        pltpu.make_async_copy(fine_hbm, fine_ref, sems.at[1]),
        pltpu.make_async_copy(left_hbm.at[sub], left_ref, sems.at[2]),
        pltpu.make_async_copy(wave_hbm, wave_ref, sems.at[3]),
        pltpu.make_async_copy(back_hbm.at[sub], back_ref, sems.at[4]),
    ]
    for copy in copies:
        copy.start()
    copies[0].wait()
    copies[1].wait()
    fine_re, fine_im = fine_ref[0], fine_ref[1]
    for number in range(coarse_ref.shape[1]):
        tab_re = coarse_ref[0, number : number + 1]
        tab_im = coarse_ref[1, number : number + 1]
        cut = slice(number * STEP, (number + 1) * STEP)
        turn_ref[0, cut] = fine_re * tab_re - fine_im * tab_im
        turn_ref[1, cut] = fine_re * tab_im + fine_im * tab_re
    for copy in copies[2:]:
        copy.wait()


def run_tables(group, tables):
    left, back, wave, coarse, fine = tables
    own = left.shape[1] // 2
    return pl.pallas_call(
        functools.partial(tables_kernel, group),
        out_shape=(
            jax.ShapeDtypeStruct(left.shape[1:], BF),
            jax.ShapeDtypeStruct(back.shape[1:], BF),
            jax.ShapeDtypeStruct(wave.shape, BF),
            jax.ShapeDtypeStruct((2, own, COLS), F32),
        ),
        in_specs=[HBM] * 5,
        out_specs=(VMEM,) * 4,
        scratch_shapes=[
            pltpu.VMEM(coarse.shape[1:], F32),
            pltpu.VMEM(fine.shape, F32),
            pltpu.SemaphoreType.DMA((5,)),
        ],
        compiler_params=params(40),
        cost_estimate=cost(3e9),
        name="load_tables",
    )(*tables)


def prepare_kernel(chans, group, *refs):
    filter_hbm, key_hbm, value_hbm = refs[:3]
    outs = refs[3 : 3 + chans]
    filter_ref, key_ref, value_ref, pair_ref, sems = refs[3 + chans :]
    home = lax.axis_index("ctx") // group
    rows = pair_ref.shape[2]
    step = rows // PIECES
    copies = []
    for number in range(PIECES):
        cut = slice(number * step * COLS, (number + 1) * step * COLS)
        for kind, (source, target) in enumerate(
            ((filter_hbm, filter_ref), (key_hbm, key_ref), (value_hbm, value_ref))
        ):
            copy = pltpu.make_async_copy(
                source.at[:, cut], target.at[:, cut], sems.at[kind, number]
            )
            copy.start()
            copies.append(copy)
    shape = (chans, 16, COLS)
    for number in range(PIECES):
        for copy in copies[3 * number : 3 * number + 3]:
            copy.wait()
        for first in range(number * step, (number + 1) * step, 16):
            cut = slice(first * COLS, (first + 16) * COLS)
            pair_ref[:, 0, first : first + 16] = filter_ref[:, cut].astype(BF).reshape(shape)
            signal = key_ref[:, cut].astype(F32) * value_ref[:, cut].astype(F32)
            pair_ref[:, 1, first : first + 16] = signal.astype(BF).reshape(shape)
    for rel in range(chans):
        outs[rel][...] = pair_ref[home ^ rel]


def run_prepare(long_filter, key, value, group):
    chans, tok_count = key.shape
    rows = tok_count // COLS
    return pl.pallas_call(
        functools.partial(prepare_kernel, chans, group),
        out_shape=(jax.ShapeDtypeStruct((2, rows, COLS), BF),) * chans,
        in_specs=[HBM] * 3,
        out_specs=(VMEM,) * chans,
        scratch_shapes=[
            pltpu.VMEM((chans, tok_count), F32),
            pltpu.VMEM((chans, tok_count), BF),
            pltpu.VMEM((chans, tok_count), BF),
            pltpu.VMEM((chans, 2, rows, COLS), BF),
            pltpu.SemaphoreType.DMA((3, PIECES)),
        ],
        compiler_params=params(60),
        cost_estimate=cost(4 * chans * tok_count),
        name="prepare_blocks",
    )(long_filter, key, value)


def finish_kernel(first_ref, acc_ref, got_ref, out_hbm, out_ref, sems):
    feats, rows, _ = first_ref.shape
    step = rows // PIECES
    copies = []
    for number in range(PIECES):
        for row in range(number * step, (number + 1) * step, 16):
            cut = slice(row, row + 16)
            second = (acc_ref[:, cut] + got_ref[:, cut].astype(F32)).astype(BF)
            whole = jnp.concatenate([first_ref[:, cut], second], 2)
            out_ref[:, row * COLS : (row + 16) * COLS] = whole.reshape(feats, 16 * COLS)
        cut = slice(number * step * COLS, (number + 1) * step * COLS)
        copy = pltpu.make_async_copy(out_ref.at[:, cut], out_hbm.at[:, cut], sems.at[number])
        copy.start()
        copies.append(copy)
    for copy in copies:
        copy.wait()


def run_finish(first, acc, got):
    feats, rows, _ = first.shape
    return pl.pallas_call(
        finish_kernel,
        out_shape=jax.ShapeDtypeStruct((feats, rows * COLS), BF),
        in_specs=[VMEM] * 3,
        out_specs=HBM,
        scratch_shapes=[
            pltpu.VMEM((feats, rows * COLS), BF),
            pltpu.SemaphoreType.DMA((PIECES,)),
        ],
        compiler_params=params(12),
        cost_estimate=cost(feats * rows * COLS),
        name="finish",
    )(first, acc, got)


def spectrum_kernel(chans, group, scale, *refs):
    count = chans * group
    blocks = refs[:count]
    left_ref, wave_ref, turn_ref, prod_ref, out_ref = refs[count : count + 5]
    x_ref, mid_ref, spec_ref = refs[count + 5 :]
    rows = blocks[0].shape[1]
    own = mid_ref.shape[0]
    home = lax.axis_index("ctx") // group
    for step in range(group):
        for rel in range(chans):
            first = pl.multiple_of((step * chans + (home ^ rel)) * rows, rows)
            for kind in range(2):
                x_ref[kind, pl.ds(first, rows)] = blocks[step * chans + rel][kind]
    for kind in range(2):
        for tile in range(0, COLS, 256):
            cut = slice(tile, tile + 256)
            val_re = dot(left_ref[:own], x_ref[kind, :, cut])
            val_im = dot(left_ref[own:], x_ref[kind, :, cut])
            tab_re, tab_im = turn_ref[0, :, cut], turn_ref[1, :, cut]
            mid_re = (val_re * tab_re - val_im * tab_im).astype(BF)
            mid_ref[:, cut] = mid_re
            mid_ref[:, COLS + tile : COLS + tile + 256] = (
                val_re * tab_im + val_im * tab_re
            ).astype(BF)
            mid_ref[:, 2 * COLS + tile : 2 * COLS + tile + 256] = -mid_re
        for tile in range(0, COLS, 256):
            cut = slice(tile, tile + 256)
            out_re = dot(mid_ref[:, : 2 * COLS], wave_ref[:, cut])
            out_im = dot(mid_ref[:, COLS:], wave_ref[:, cut])
            if kind == 0:
                spec_ref[0, :, cut] = out_re * scale
                spec_ref[1, :, cut] = out_im * scale
            else:
                fil_re, fil_im = spec_ref[0, :, cut], spec_ref[1, :, cut]
                prod_im = (out_re * fil_im + out_im * fil_re).astype(BF)
                prod_ref[:, cut] = prod_im
                prod_ref[:, COLS + tile : COLS + tile + 256] = (
                    out_re * fil_re - out_im * fil_im
                ).astype(BF)
                prod_ref[:, 2 * COLS + tile : 2 * COLS + tile + 256] = -prod_im
    back_stage(CUTS[0], CUTS[1], prod_ref, wave_ref, turn_ref, out_ref)


def back_stage(low, high, prod_ref, wave_ref, turn_ref, out_ref):
    own = prod_ref.shape[0]
    cut = slice(low, high)
    val_im = dot(prod_ref[:, : 2 * COLS], wave_ref[:, cut])
    val_re = dot(prod_ref[:, COLS:], wave_ref[:, cut])
    tab_re, tab_im = turn_ref[0, :, cut], turn_ref[1, :, cut]
    out_ref[:own] = (val_re * tab_re + val_im * tab_im).astype(BF)
    out_ref[own:] = (val_im * tab_re - val_re * tab_im).astype(BF)


def position_kernel(chans, group, *refs):
    parts, table_ref = refs[:group], refs[group]
    outs, sum_ref = refs[group + 1 : group + 1 + chans], refs[group + 1 + chans]
    home = lax.axis_index("ctx") // group
    depth = parts[0].shape[0]
    total = dot(table_ref[:, :depth], parts[0][...])
    for step in range(1, group):
        total += dot(table_ref[:, step * depth : (step + 1) * depth], parts[step][...])
    sum_ref[...] = total.astype(BF)
    rows = outs[0].shape[0]
    for rel in range(chans):
        outs[rel][...] = sum_ref[pl.ds(pl.multiple_of((home ^ rel) * rows, rows), rows)]


def gate_kernel(chans, group, low, high, *refs):
    parts = refs[:chans]
    query_ref, key_ref, value_ref, gain_ref, out_ref = refs[chans:]
    cut = slice(low, high)
    home = lax.axis_index("ctx") // group
    for rel in range(chans):
        chan = home ^ rel
        signal = key_ref[chan, :, cut].astype(F32) * value_ref[chan, :, cut].astype(F32)
        total = parts[rel][...].astype(F32) + gain_ref[chan] * signal
        out_ref[chan] = (query_ref[chan, :, cut].astype(F32) * total).astype(BF)


def run_spectrum(blocks, chans, group, tables, scale):
    left, _, wave, turn = tables
    own, big = left.shape[0] // 2, left.shape[1]
    return pl.pallas_call(
        functools.partial(spectrum_kernel, chans, group, scale),
        out_shape=(
            jax.ShapeDtypeStruct((own, 3 * COLS), BF),
            jax.ShapeDtypeStruct((2 * own, CUTS[1] - CUTS[0]), BF),
        ),
        in_specs=[VMEM] * (len(blocks) + 3),
        out_specs=(VMEM, VMEM),
        scratch_shapes=[
            pltpu.VMEM((2, big, COLS), BF),
            pltpu.VMEM((own, 3 * COLS), BF),
            pltpu.VMEM((2, own, COLS), F32),
        ],
        compiler_params=params(20),
        cost_estimate=cost(8 * own * COLS * (big + 3 * COLS)),
        name="spectrum_product",
    )(*blocks, left, wave, turn)


def run_back(prod, tables, low, high):
    _, _, wave, turn = tables
    own = prod.shape[0]
    return pl.pallas_call(
        functools.partial(back_stage, low, high),
        out_shape=jax.ShapeDtypeStruct((2 * own, high - low), BF),
        in_specs=[VMEM] * 3,
        out_specs=VMEM,
        compiler_params=params(12),
        cost_estimate=cost(8 * own * COLS * (high - low)),
        name="back_columns",
    )(prod, wave, turn)


def run_position(parts, chans, group, table):
    out_rows, depth = table.shape
    cols = parts[0].shape[1]
    rows = out_rows // chans
    return pl.pallas_call(
        functools.partial(position_kernel, chans, group),
        out_shape=(jax.ShapeDtypeStruct((rows, cols), BF),) * chans,
        in_specs=[VMEM] * (group + 1),
        out_specs=(VMEM,) * chans,
        scratch_shapes=[pltpu.VMEM((out_rows, cols), BF)],
        compiler_params=params(12),
        cost_estimate=cost(2 * out_rows * depth * cols),
        name="back_positions",
    )(*parts, table)


def run_gate(parts, query, key, value, gain, group, low, high):
    chans, rows, _ = query.shape
    return pl.pallas_call(
        functools.partial(gate_kernel, chans, group, low, high),
        out_shape=jax.ShapeDtypeStruct((chans, rows, high - low), BF),
        in_specs=[VMEM] * (chans + 3) + [SMEM],
        out_specs=VMEM,
        compiler_params=params(12),
        cost_estimate=cost(4 * chans * rows * (high - low)),
        name="gate",
    )(*parts, query, key, value, gain)


def mix_kernel(chans, slots, outputs, plane_ref, weight_ref, *refs):
    count = len(slots)
    feats = refs[count].shape[0]

    @pl.loop(0, refs[0].shape[1] // 16)
    def _(index):
        rows = pl.ds(pl.multiple_of(index * 16, 16), 16)
        sums = [[None] * feats for _ in outputs]
        for slot, ref in zip(slots, refs[:count]):
            for chan in range(chans):
                value = ref[chan, rows].astype(F32)
                row = plane_ref[slot] * chans + chan
                for out, total in zip(outputs, sums):
                    for feat in range(feats):
                        term = value * weight_ref[row, plane_ref[out[0]] * feats + feat]
                        total[feat] = term if total[feat] is None else total[feat] + term
        for ref, total in zip(refs[count:], sums):
            for feat in range(feats):
                ref[feat, rows] = total[feat].astype(ref.dtype)


def run_mix(planes, weight, slots, outputs, values):
    chans, rows, cols = values[0].shape
    feats = weight.shape[1] // 4
    size = feats * rows * cols
    return pl.pallas_call(
        functools.partial(mix_kernel, chans, slots, outputs),
        out_shape=tuple(jax.ShapeDtypeStruct((feats, rows, cols), out[1]) for out in outputs),
        in_specs=[SMEM, SMEM] + [VMEM] * len(slots),
        out_specs=(VMEM,) * len(outputs),
        compiler_params=params(12),
        cost_estimate=cost(2 * chans * len(slots) * len(outputs) * size),
        name="mix_features",
    )(planes, weight, *values)


def line_mix(gated, out_weight):
    plane = lax.axis_index("tp")
    near = plane < 2
    planes = jnp.stack(
        [plane, jnp.where(near, 2, 1), jnp.where(near, 3, 0), jnp.where(near, 0, 3), plane ^ 1]
    ).astype(jnp.int32)
    own_at, mid_at, far_at, edge_at, pair_at = range(5)
    weight = out_weight.astype(F32)
    mix = functools.partial(run_mix, planes, weight)
    swapped, gathered = gated
    far = lax.ppermute(gathered, "tp", [(0, 2), (3, 1)])
    mid = lax.ppermute(gathered, "tp", [(1, 2), (2, 1)])
    pair = lax.ppermute(swapped, "tp", [(0, 1), (1, 0), (2, 3), (3, 2)])
    to_mid, to_far = mix((own_at, pair_at), ((mid_at, BF), (far_at, BF)), (swapped, pair))
    from_far = lax.ppermute(to_far, "tp", [(1, 3), (2, 0)])
    from_mid = lax.ppermute(to_mid, "tp", [(1, 2), (2, 1)])
    gathered, _ = lax.optimization_barrier((gathered, to_mid))
    edge = lax.ppermute(gathered, "tp", [(0, 1), (3, 2)])
    far, mid, to_mid, to_far = lax.optimization_barrier((far, mid, to_mid, to_far))
    (to_edge,) = mix((own_at, far_at, mid_at), ((edge_at, BF),), (gathered, far, mid))
    from_edge = lax.ppermute(to_edge, "tp", [(2, 3), (1, 0)])
    (acc_swapped,) = mix((own_at, pair_at), ((own_at, F32),), (swapped, pair))
    (acc_gathered,) = mix(
        (own_at, far_at, mid_at, edge_at), ((own_at, F32),), (gathered, far, mid, edge)
    )
    done = (acc_swapped + from_far.astype(F32) + from_mid.astype(F32)).astype(BF)
    done, acc_gathered = lax.optimization_barrier((done, acc_gathered))
    return run_finish(done, acc_gathered, from_edge)


def gather_mix(gated, out_weight):
    plane = lax.axis_index("tp")
    outs = out_weight.shape[1] // lax.axis_size("tp")
    own_cols = lax.dynamic_slice_in_dim(out_weight, plane * outs, outs, 1)
    mixed = [
        jnp.einsum(
            "co,crl->orl",
            own_cols,
            lax.all_gather(own, "tp", axis=0, tiled=True),
            preferred_element_type=F32,
        ).astype(BF)
        for own in gated
    ]
    return jnp.concatenate(mixed, 2).reshape(outs, -1)


def local(query_gate, key_branch, value_branch, long_filter, skip_gain, out_weight):
    ctx_count = lax.axis_size("ctx")
    chans, tok_count = query_gate.shape
    rows = tok_count // COLS
    group = ctx_count // chans
    length = ctx_count * tok_count
    shape = (chans, rows, COLS)
    tables = run_tables(group, make_tables(ctx_count, group, chans, rows))

    def swap(values):
        got = [values[0]]
        for rel in range(1, chans):
            pairs = [
                (group * chip + core, group * (chip ^ rel) + core)
                for chip in range(chans)
                for core in range(group)
            ]
            got.append(lax.ppermute(values[rel], "ctx", pairs))
        return got

    def shift(value, step):
        pairs = [
            (group * chip + core, group * chip + (core + step) % group)
            for chip in range(chans)
            for core in range(group)
        ]
        return lax.ppermute(value, "ctx", pairs)

    query = query_gate.reshape(shape)
    key = key_branch.reshape(shape)
    value = value_branch.reshape(shape)
    blocks = run_prepare(long_filter, key_branch, value_branch, group)
    blocks = swap(list(blocks))
    blocks[-1], tables = lax.optimization_barrier((blocks[-1], tables))
    blocks += [shift(part, -step) for step in range(1, group) for part in blocks]
    spans = list(zip(CUTS[:-1], CUTS[1:]))
    prod, back = run_spectrum(blocks, chans, group, tables, 1.0 / length)
    backs = [back] + [run_back(prod, tables, *span) for span in spans[1:]]
    places = []
    for back in backs:
        parts = [back] + [shift(back, -step) for step in range(1, group)]
        places.append(run_position(parts, chans, group, tables[1]))
    gated = []
    parts = swap(list(places[0]))
    for number, span in enumerate(spans):
        if number + 1 < len(spans):
            parts, _ = lax.optimization_barrier((parts, places[number + 1]))
        if number > 0:
            parts, gated[-1] = lax.optimization_barrier((parts, gated[-1]))
        gated.append(run_gate(parts, query, key, value, skip_gain, group, *span))
        if number + 1 < len(spans):
            parts = swap(list(places[number + 1]))
    return (line_mix if lax.axis_size("tp") == 4 else gather_mix)(gated, out_weight)


def solution(mesh):
    placed = (P("tp", "ctx"), P("tp", "ctx"), P("tp", "ctx"), P("tp", "ctx"), P("tp"), P())
    return jax.shard_map(
        local, mesh=mesh, in_specs=placed, out_specs=P("tp", "ctx"), check_vma=False
    )
```

```python
import functools

import jax
import jax.numpy as jnp
import numpy as np
from jax import lax
from jax.experimental import pallas as pl
from jax.experimental.pallas import tpu as pltpu
from jax.sharding import PartitionSpec as P

COLS = 512
STEP = 32
PIECES = 4
CUTS = (0, 256, 512)
BF = jnp.bfloat16
F32 = jnp.float32
VMEM = pl.BlockSpec(memory_space=pltpu.VMEM)
SMEM = pl.BlockSpec(memory_space=pltpu.SMEM)
HBM = pl.BlockSpec(memory_space=pltpu.HBM)


def make_tables(ctx_count, group, chans, rows):
    big = ctx_count * rows
    own = big // group
    length = big * COLS
    k_one = np.arange(big, dtype=np.int64)
    n_one = np.arange(big, dtype=np.int64)
    angle = 2 * np.pi / (4 * big) * ((4 * k_one[:, None] + 1) * n_one[None, :] % (4 * big))
    both = np.stack([np.cos(angle), -np.sin(angle)], 0)
    both = both.reshape(2, group, own, chans, group, rows)
    left = np.empty((group, 2 * own, group, chans * rows))
    back_left = np.empty((group, chans * rows, group, 2 * own))
    for sub in range(group):
        for step in range(group):
            other = (sub + step) % group
            left[sub, :, step] = both[:, sub, :, :, other].reshape(2 * own, -1)
            back_left[sub, :, step] = both[:, other, :, :, sub].reshape(2 * own, -1).T
    n_two = np.arange(COLS, dtype=np.int64)
    coarse = STEP * np.arange(big // STEP, dtype=np.int64)
    fine = np.arange(STEP, dtype=np.int64)
    angle = 2 * np.pi / (4 * length) * (4 * coarse[:, None] * n_two[None, :] % (4 * length))
    coarse = np.stack([np.cos(angle), -np.sin(angle)], 0).reshape(2, group, own // STEP, COLS)
    coarse = np.ascontiguousarray(coarse.transpose(1, 0, 2, 3))
    angle = 2 * np.pi / (4 * length) * ((4 * fine[:, None] + 1) * n_two[None, :] % (4 * length))
    fine = np.stack([np.cos(angle), -np.sin(angle)], 0)
    angle = 2 * np.pi / COLS * (n_two[:, None] * n_two[None, :] % COLS)
    return (
        left.reshape(group, 2 * own, big).astype(BF),
        back_left.reshape(group, chans * rows, 2 * big).astype(BF),
        np.concatenate([np.cos(angle), np.sin(angle)], 0).astype(BF),
        coarse.astype(np.float32),
        fine.astype(np.float32),
    )


def dot(left, right):
    return jnp.dot(left, right, preferred_element_type=F32)


def cost(flops):
    return pl.CostEstimate(flops=int(flops), bytes_accessed=0, transcendentals=0)


def params(mib):
    return pltpu.CompilerParams(vmem_limit_bytes=mib * 2**20)


def tables_kernel(group, *refs):
    left_hbm, back_hbm, wave_hbm, coarse_hbm, fine_hbm = refs[:5]
    left_ref, back_ref, wave_ref, turn_ref, coarse_ref, fine_ref, sems = refs[5:]
    sub = lax.rem(lax.axis_index("ctx"), group)
    copies = [
        pltpu.make_async_copy(coarse_hbm.at[sub], coarse_ref, sems.at[0]),
        pltpu.make_async_copy(fine_hbm, fine_ref, sems.at[1]),
        pltpu.make_async_copy(left_hbm.at[sub], left_ref, sems.at[2]),
        pltpu.make_async_copy(wave_hbm, wave_ref, sems.at[3]),
        pltpu.make_async_copy(back_hbm.at[sub], back_ref, sems.at[4]),
    ]
    for copy in copies:
        copy.start()
    copies[0].wait()
    copies[1].wait()
    fine_re, fine_im = fine_ref[0], fine_ref[1]
    for number in range(coarse_ref.shape[1]):
        tab_re = coarse_ref[0, number : number + 1]
        tab_im = coarse_ref[1, number : number + 1]
        cut = slice(number * STEP, (number + 1) * STEP)
        turn_ref[0, cut] = fine_re * tab_re - fine_im * tab_im
        turn_ref[1, cut] = fine_re * tab_im + fine_im * tab_re
    for copy in copies[2:]:
        copy.wait()


def run_tables(group, tables):
    left, back, wave, coarse, fine = tables
    own = left.shape[1] // 2
    return pl.pallas_call(
        functools.partial(tables_kernel, group),
        out_shape=(
            jax.ShapeDtypeStruct(left.shape[1:], BF),
            jax.ShapeDtypeStruct(back.shape[1:], BF),
            jax.ShapeDtypeStruct(wave.shape, BF),
            jax.ShapeDtypeStruct((2, own, COLS), F32),
        ),
        in_specs=[HBM] * 5,
        out_specs=(VMEM,) * 4,
        scratch_shapes=[
            pltpu.VMEM(coarse.shape[1:], F32),
            pltpu.VMEM(fine.shape, F32),
            pltpu.SemaphoreType.DMA((5,)),
        ],
        compiler_params=params(40),
        cost_estimate=cost(3e9),
        name="load_tables",
    )(*tables)


def prepare_kernel(chans, group, *refs):
    filter_hbm, key_hbm, value_hbm = refs[:3]
    outs = refs[3 : 3 + chans]
    filter_ref, key_ref, value_ref, pair_ref, sems = refs[3 + chans :]
    home = lax.axis_index("ctx") // group
    rows = pair_ref.shape[2]
    step = rows // PIECES
    copies = []
    for number in range(PIECES):
        cut = slice(number * step * COLS, (number + 1) * step * COLS)
        for kind, (source, target) in enumerate(
            ((filter_hbm, filter_ref), (key_hbm, key_ref), (value_hbm, value_ref))
        ):
            copy = pltpu.make_async_copy(
                source.at[:, cut], target.at[:, cut], sems.at[kind, number]
            )
            copy.start()
            copies.append(copy)
    shape = (chans, 16, COLS)
    for number in range(PIECES):
        for copy in copies[3 * number : 3 * number + 3]:
            copy.wait()
        for first in range(number * step, (number + 1) * step, 16):
            cut = slice(first * COLS, (first + 16) * COLS)
            pair_ref[:, 0, first : first + 16] = filter_ref[:, cut].astype(BF).reshape(shape)
            signal = key_ref[:, cut].astype(F32) * value_ref[:, cut].astype(F32)
            pair_ref[:, 1, first : first + 16] = signal.astype(BF).reshape(shape)
    for rel in range(chans):
        outs[rel][...] = pair_ref[home ^ rel]


def run_prepare(long_filter, key, value, group):
    chans, tok_count = key.shape
    rows = tok_count // COLS
    return pl.pallas_call(
        functools.partial(prepare_kernel, chans, group),
        out_shape=(jax.ShapeDtypeStruct((2, rows, COLS), BF),) * chans,
        in_specs=[HBM] * 3,
        out_specs=(VMEM,) * chans,
        scratch_shapes=[
            pltpu.VMEM((chans, tok_count), F32),
            pltpu.VMEM((chans, tok_count), BF),
            pltpu.VMEM((chans, tok_count), BF),
            pltpu.VMEM((chans, 2, rows, COLS), BF),
            pltpu.SemaphoreType.DMA((3, PIECES)),
        ],
        compiler_params=params(60),
        cost_estimate=cost(4 * chans * tok_count),
        name="prepare_blocks",
    )(long_filter, key, value)


def finish_kernel(first_ref, acc_ref, got_ref, out_hbm, out_ref, sems):
    feats, rows, _ = first_ref.shape
    step = rows // PIECES
    copies = []
    for number in range(PIECES):
        for row in range(number * step, (number + 1) * step, 16):
            cut = slice(row, row + 16)
            second = (acc_ref[:, cut] + got_ref[:, cut].astype(F32)).astype(BF)
            whole = jnp.concatenate([first_ref[:, cut], second], 2)
            out_ref[:, row * COLS : (row + 16) * COLS] = whole.reshape(feats, 16 * COLS)
        cut = slice(number * step * COLS, (number + 1) * step * COLS)
        copy = pltpu.make_async_copy(out_ref.at[:, cut], out_hbm.at[:, cut], sems.at[number])
        copy.start()
        copies.append(copy)
    for copy in copies:
        copy.wait()


def run_finish(first, acc, got):
    feats, rows, _ = first.shape
    return pl.pallas_call(
        finish_kernel,
        out_shape=jax.ShapeDtypeStruct((feats, rows * COLS), BF),
        in_specs=[VMEM] * 3,
        out_specs=HBM,
        scratch_shapes=[
            pltpu.VMEM((feats, rows * COLS), BF),
            pltpu.SemaphoreType.DMA((PIECES,)),
        ],
        compiler_params=params(12),
        cost_estimate=cost(feats * rows * COLS),
        name="finish",
    )(first, acc, got)


def early_kernel(chans, group, early, late, *refs):
    count = len(early) * group
    blocks, (left_ref, sum_ref, rest_ref) = refs[:count], refs[count : count + 3]
    x_ref, part_ref = refs[count + 3 :]
    rows = blocks[0].shape[1]
    home = lax.axis_index("ctx") // group
    for rels, target in ((early, part_ref), (late, rest_ref)):
        for number in range(len(rels) * group):
            step, rel = number // len(rels), rels[number % len(rels)]
            first = pl.multiple_of((step * chans + (home ^ rel)) * rows, rows)
            target[:, number * rows : (number + 1) * rows] = left_ref[:, pl.ds(first, rows)]
    for number, block in enumerate(blocks):
        for kind in range(2):
            x_ref[kind, number * rows : (number + 1) * rows] = block[kind]
    half = sum_ref.shape[1] // 2
    for kind in range(2):
        for tile in range(0, COLS, 256):
            cut = slice(tile, tile + 256)
            sum_ref[kind, :half, cut] = dot(part_ref[:half], x_ref[kind, :, cut])
            sum_ref[kind, half:, cut] = dot(part_ref[half:], x_ref[kind, :, cut])


def run_early(blocks, chans, group, early, late, left):
    size, big = left.shape
    rows = big // (chans * group)
    width, rest = len(early) * group * rows, len(late) * group * rows
    return pl.pallas_call(
        functools.partial(early_kernel, chans, group, early, late),
        out_shape=(
            jax.ShapeDtypeStruct((2, size, COLS), F32),
            jax.ShapeDtypeStruct((size, rest), BF),
        ),
        in_specs=[VMEM] * (len(blocks) + 1),
        out_specs=(VMEM, VMEM),
        scratch_shapes=[pltpu.VMEM((2, width, COLS), BF), pltpu.VMEM((size, width), BF)],
        compiler_params=params(12),
        cost_estimate=cost(4 * size * COLS * width),
        name="early_stage",
    )(*blocks, left)


def spectrum_kernel(scale, *refs):
    count = len(refs) - 9
    blocks = refs[:count]
    sum_ref, left_ref, wave_ref, turn_ref, prod_ref, out_ref = refs[count : count + 6]
    x_ref, mid_ref, spec_ref = refs[count + 6 :]
    rows = blocks[0].shape[1]
    own = mid_ref.shape[0]
    for number, block in enumerate(blocks):
        for kind in range(2):
            x_ref[kind, number * rows : (number + 1) * rows] = block[kind]
    for kind in range(2):
        for tile in range(0, COLS, 256):
            cut = slice(tile, tile + 256)
            val_re = dot(left_ref[:own], x_ref[kind, :, cut]) + sum_ref[kind, :own, cut]
            val_im = dot(left_ref[own:], x_ref[kind, :, cut]) + sum_ref[kind, own:, cut]
            tab_re, tab_im = turn_ref[0, :, cut], turn_ref[1, :, cut]
            mid_re = (val_re * tab_re - val_im * tab_im).astype(BF)
            mid_ref[:, cut] = mid_re
            mid_ref[:, COLS + tile : COLS + tile + 256] = (
                val_re * tab_im + val_im * tab_re
            ).astype(BF)
            mid_ref[:, 2 * COLS + tile : 2 * COLS + tile + 256] = -mid_re
        for tile in range(0, COLS, 256):
            cut = slice(tile, tile + 256)
            out_re = dot(mid_ref[:, : 2 * COLS], wave_ref[:, cut])
            out_im = dot(mid_ref[:, COLS:], wave_ref[:, cut])
            if kind == 0:
                spec_ref[0, :, cut] = out_re * scale
                spec_ref[1, :, cut] = out_im * scale
            else:
                fil_re, fil_im = spec_ref[0, :, cut], spec_ref[1, :, cut]
                prod_im = (out_re * fil_im + out_im * fil_re).astype(BF)
                prod_ref[:, cut] = prod_im
                prod_ref[:, COLS + tile : COLS + tile + 256] = (
                    out_re * fil_re - out_im * fil_im
                ).astype(BF)
                prod_ref[:, 2 * COLS + tile : 2 * COLS + tile + 256] = -prod_im
    back_stage(CUTS[0], CUTS[1], prod_ref, wave_ref, turn_ref, out_ref)


def back_stage(low, high, prod_ref, wave_ref, turn_ref, out_ref):
    own = prod_ref.shape[0]
    cut = slice(low, high)
    val_im = dot(prod_ref[:, : 2 * COLS], wave_ref[:, cut])
    val_re = dot(prod_ref[:, COLS:], wave_ref[:, cut])
    tab_re, tab_im = turn_ref[0, :, cut], turn_ref[1, :, cut]
    out_ref[:own] = (val_re * tab_re + val_im * tab_im).astype(BF)
    out_ref[own:] = (val_im * tab_re - val_re * tab_im).astype(BF)


def position_kernel(chans, group, *refs):
    parts, table_ref = refs[:group], refs[group]
    outs, sum_ref = refs[group + 1 : group + 1 + chans], refs[group + 1 + chans]
    home = lax.axis_index("ctx") // group
    depth = parts[0].shape[0]
    total = dot(table_ref[:, :depth], parts[0][...])
    for step in range(1, group):
        total += dot(table_ref[:, step * depth : (step + 1) * depth], parts[step][...])
    sum_ref[...] = total.astype(BF)
    rows = outs[0].shape[0]
    for rel in range(chans):
        outs[rel][...] = sum_ref[pl.ds(pl.multiple_of((home ^ rel) * rows, rows), rows)]


def gate_kernel(chans, group, low, high, *refs):
    parts = refs[:chans]
    query_ref, key_ref, value_ref, gain_ref, out_ref = refs[chans:]
    cut = slice(low, high)
    home = lax.axis_index("ctx") // group
    for rel in range(chans):
        chan = home ^ rel
        signal = key_ref[chan, :, cut].astype(F32) * value_ref[chan, :, cut].astype(F32)
        total = parts[rel][...].astype(F32) + gain_ref[chan] * signal
        out_ref[chan] = (query_ref[chan, :, cut].astype(F32) * total).astype(BF)


def run_spectrum(blocks, sums, left, tables, scale):
    _, _, wave, turn = tables
    own, width = left.shape[0] // 2, left.shape[1]
    return pl.pallas_call(
        functools.partial(spectrum_kernel, scale),
        out_shape=(
            jax.ShapeDtypeStruct((own, 3 * COLS), BF),
            jax.ShapeDtypeStruct((2 * own, CUTS[1] - CUTS[0]), BF),
        ),
        in_specs=[VMEM] * (len(blocks) + 4),
        out_specs=(VMEM, VMEM),
        scratch_shapes=[
            pltpu.VMEM((2, width, COLS), BF),
            pltpu.VMEM((own, 3 * COLS), BF),
            pltpu.VMEM((2, own, COLS), F32),
        ],
        compiler_params=params(20),
        cost_estimate=cost(8 * own * COLS * (width + 3 * COLS)),
        name="spectrum_product",
    )(*blocks, sums, left, wave, turn)


def run_back(prod, tables, low, high):
    _, _, wave, turn = tables
    own = prod.shape[0]
    return pl.pallas_call(
        functools.partial(back_stage, low, high),
        out_shape=jax.ShapeDtypeStruct((2 * own, high - low), BF),
        in_specs=[VMEM] * 3,
        out_specs=VMEM,
        compiler_params=params(12),
        cost_estimate=cost(8 * own * COLS * (high - low)),
        name="back_columns",
    )(prod, wave, turn)


def run_position(parts, chans, group, table):
    out_rows, depth = table.shape
    cols = parts[0].shape[1]
    rows = out_rows // chans
    return pl.pallas_call(
        functools.partial(position_kernel, chans, group),
        out_shape=(jax.ShapeDtypeStruct((rows, cols), BF),) * chans,
        in_specs=[VMEM] * (group + 1),
        out_specs=(VMEM,) * chans,
        scratch_shapes=[pltpu.VMEM((out_rows, cols), BF)],
        compiler_params=params(12),
        cost_estimate=cost(2 * out_rows * depth * cols),
        name="back_positions",
    )(*parts, table)


def run_gate(parts, query, key, value, gain, group, low, high):
    chans, rows, _ = query.shape
    return pl.pallas_call(
        functools.partial(gate_kernel, chans, group, low, high),
        out_shape=jax.ShapeDtypeStruct((chans, rows, high - low), BF),
        in_specs=[VMEM] * (chans + 3) + [SMEM],
        out_specs=VMEM,
        compiler_params=params(12),
        cost_estimate=cost(4 * chans * rows * (high - low)),
        name="gate",
    )(*parts, query, key, value, gain)


def mix_kernel(chans, slots, outputs, plane_ref, weight_ref, *refs):
    count = len(slots)
    feats = refs[count].shape[0]

    @pl.loop(0, refs[0].shape[1] // 16)
    def _(index):
        rows = pl.ds(pl.multiple_of(index * 16, 16), 16)
        sums = [[None] * feats for _ in outputs]
        for slot, ref in zip(slots, refs[:count]):
            for chan in range(chans):
                value = ref[chan, rows].astype(F32)
                row = plane_ref[slot] * chans + chan
                for out, total in zip(outputs, sums):
                    for feat in range(feats):
                        term = value * weight_ref[row, plane_ref[out[0]] * feats + feat]
                        total[feat] = term if total[feat] is None else total[feat] + term
        for ref, total in zip(refs[count:], sums):
            for feat in range(feats):
                ref[feat, rows] = total[feat].astype(ref.dtype)


def run_mix(planes, weight, slots, outputs, values):
    chans, rows, cols = values[0].shape
    feats = weight.shape[1] // 4
    size = feats * rows * cols
    return pl.pallas_call(
        functools.partial(mix_kernel, chans, slots, outputs),
        out_shape=tuple(jax.ShapeDtypeStruct((feats, rows, cols), out[1]) for out in outputs),
        in_specs=[SMEM, SMEM] + [VMEM] * len(slots),
        out_specs=(VMEM,) * len(outputs),
        compiler_params=params(12),
        cost_estimate=cost(2 * chans * len(slots) * len(outputs) * size),
        name="mix_features",
    )(planes, weight, *values)


def line_mix(gated, out_weight):
    plane = lax.axis_index("tp")
    near = plane < 2
    planes = jnp.stack(
        [plane, jnp.where(near, 2, 1), jnp.where(near, 3, 0), jnp.where(near, 0, 3), plane ^ 1]
    ).astype(jnp.int32)
    own_at, mid_at, far_at, edge_at, pair_at = range(5)
    weight = out_weight.astype(F32)
    mix = functools.partial(run_mix, planes, weight)
    swapped, gathered = gated
    far = lax.ppermute(gathered, "tp", [(0, 2), (3, 1)])
    mid = lax.ppermute(gathered, "tp", [(1, 2), (2, 1)])
    pair = lax.ppermute(swapped, "tp", [(0, 1), (1, 0), (2, 3), (3, 2)])
    to_mid, to_far = mix((own_at, pair_at), ((mid_at, BF), (far_at, BF)), (swapped, pair))
    from_far = lax.ppermute(to_far, "tp", [(1, 3), (2, 0)])
    from_mid = lax.ppermute(to_mid, "tp", [(1, 2), (2, 1)])
    gathered, _ = lax.optimization_barrier((gathered, to_mid))
    edge = lax.ppermute(gathered, "tp", [(0, 1), (3, 2)])
    far, mid, to_mid, to_far = lax.optimization_barrier((far, mid, to_mid, to_far))
    (to_edge,) = mix((own_at, far_at, mid_at), ((edge_at, BF),), (gathered, far, mid))
    from_edge = lax.ppermute(to_edge, "tp", [(2, 3), (1, 0)])
    (acc_swapped,) = mix((own_at, pair_at), ((own_at, F32),), (swapped, pair))
    (acc_gathered,) = mix(
        (own_at, far_at, mid_at, edge_at), ((own_at, F32),), (gathered, far, mid, edge)
    )
    done = (acc_swapped + from_far.astype(F32) + from_mid.astype(F32)).astype(BF)
    done, acc_gathered = lax.optimization_barrier((done, acc_gathered))
    return run_finish(done, acc_gathered, from_edge)


def gather_mix(gated, out_weight):
    plane = lax.axis_index("tp")
    outs = out_weight.shape[1] // lax.axis_size("tp")
    own_cols = lax.dynamic_slice_in_dim(out_weight, plane * outs, outs, 1)
    mixed = [
        jnp.einsum(
            "co,crl->orl",
            own_cols,
            lax.all_gather(own, "tp", axis=0, tiled=True),
            preferred_element_type=F32,
        ).astype(BF)
        for own in gated
    ]
    return jnp.concatenate(mixed, 2).reshape(outs, -1)


def local(query_gate, key_branch, value_branch, long_filter, skip_gain, out_weight):
    ctx_count = lax.axis_size("ctx")
    chans, tok_count = query_gate.shape
    rows = tok_count // COLS
    group = ctx_count // chans
    length = ctx_count * tok_count
    shape = (chans, rows, COLS)
    tables = run_tables(group, make_tables(ctx_count, group, chans, rows))

    def swap(values):
        got = [values[0]]
        for rel in range(1, chans):
            pairs = [
                (group * chip + core, group * (chip ^ rel) + core)
                for chip in range(chans)
                for core in range(group)
            ]
            got.append(lax.ppermute(values[rel], "ctx", pairs))
        return got

    def shift(value, step):
        pairs = [
            (group * chip + core, group * chip + (core + step) % group)
            for chip in range(chans)
            for core in range(group)
        ]
        return lax.ppermute(value, "ctx", pairs)

    query = query_gate.reshape(shape)
    key = key_branch.reshape(shape)
    value = value_branch.reshape(shape)
    blocks = run_prepare(long_filter, key_branch, value_branch, group)
    blocks = swap(list(blocks))
    early = (0, chans - 1)
    late = tuple(range(1, chans - 1))
    blocks[-1], tables = lax.optimization_barrier((blocks[-1], tables))

    def share(rels, values):
        values = [values[rel] for rel in rels]
        return values + [shift(part, -step) for step in range(1, group) for part in values]

    sums, rest = run_early(share(early, blocks), chans, group, early, late, tables[0])
    blocks = share(late, blocks)
    spans = list(zip(CUTS[:-1], CUTS[1:]))
    prod, back = run_spectrum(blocks, sums, rest, tables, 1.0 / length)
    backs = [back] + [run_back(prod, tables, *span) for span in spans[1:]]
    places = []
    for back in backs:
        parts = [back] + [shift(back, -step) for step in range(1, group)]
        places.append(run_position(parts, chans, group, tables[1]))
    gated = []
    parts = swap(list(places[0]))
    for number, span in enumerate(spans):
        if number + 1 < len(spans):
            parts, _ = lax.optimization_barrier((parts, places[number + 1]))
        if number > 0:
            parts, gated[-1] = lax.optimization_barrier((parts, gated[-1]))
        gated.append(run_gate(parts, query, key, value, skip_gain, group, *span))
        if number + 1 < len(spans):
            parts = swap(list(places[number + 1]))
    return (line_mix if lax.axis_size("tp") == 4 else gather_mix)(gated, out_weight)


def solution(mesh):
    placed = (P("tp", "ctx"), P("tp", "ctx"), P("tp", "ctx"), P("tp", "ctx"), P("tp"), P())
    return jax.shard_map(
        local, mesh=mesh, in_specs=placed, out_specs=P("tp", "ctx"), check_vma=False
    )
```

```python
import functools

import jax
import jax.numpy as jnp
import numpy as np
from jax import lax
from jax.experimental import pallas as pl
from jax.experimental.pallas import tpu as pltpu
from jax.sharding import PartitionSpec as P

COLS = 512
STEP = 32
PIECES = 4
CUTS = (0, 256, 512)
BF = jnp.bfloat16
F32 = jnp.float32
VMEM = pl.BlockSpec(memory_space=pltpu.VMEM)
SMEM = pl.BlockSpec(memory_space=pltpu.SMEM)
HBM = pl.BlockSpec(memory_space=pltpu.HBM)


def make_tables(ctx_count, group, chans, rows):
    big = ctx_count * rows
    own = big // group
    length = big * COLS
    k_one = np.arange(big, dtype=np.int64)
    n_one = np.arange(big, dtype=np.int64)
    angle = 2 * np.pi / (4 * big) * ((4 * k_one[:, None] + 1) * n_one[None, :] % (4 * big))
    both = np.stack([np.cos(angle), -np.sin(angle)], 0)
    both = both.reshape(2, group, own, chans, group, rows)
    left = np.empty((group, 2 * own, group, chans * rows))
    back_left = np.empty((group, chans * rows, group, 2 * own))
    for sub in range(group):
        for step in range(group):
            other = (sub + step) % group
            left[sub, :, step] = both[:, sub, :, :, other].reshape(2 * own, -1)
            back_left[sub, :, step] = both[:, other, :, :, sub].reshape(2 * own, -1).T
    n_two = np.arange(COLS, dtype=np.int64)
    coarse = STEP * np.arange(big // STEP, dtype=np.int64)
    fine = np.arange(STEP, dtype=np.int64)
    angle = 2 * np.pi / (4 * length) * (4 * coarse[:, None] * n_two[None, :] % (4 * length))
    coarse = np.stack([np.cos(angle), -np.sin(angle)], 0).reshape(2, group, own // STEP, COLS)
    coarse = np.ascontiguousarray(coarse.transpose(1, 0, 2, 3))
    angle = 2 * np.pi / (4 * length) * ((4 * fine[:, None] + 1) * n_two[None, :] % (4 * length))
    fine = np.stack([np.cos(angle), -np.sin(angle)], 0)
    angle = 2 * np.pi / COLS * (n_two[:, None] * n_two[None, :] % COLS)
    return (
        left.reshape(group, 2 * own, big).astype(BF),
        back_left.reshape(group, chans * rows, 2 * big).astype(BF),
        np.concatenate([np.cos(angle), np.sin(angle)], 0).astype(BF),
        coarse.astype(np.float32),
        fine.astype(np.float32),
    )


def dot(left, right):
    return jnp.dot(left, right, preferred_element_type=F32)


def cost(flops):
    return pl.CostEstimate(flops=int(flops), bytes_accessed=0, transcendentals=0)


def params(mib):
    return pltpu.CompilerParams(vmem_limit_bytes=mib * 2**20)


def tables_kernel(group, *refs):
    left_hbm, back_hbm, wave_hbm, coarse_hbm, fine_hbm = refs[:5]
    left_ref, back_ref, wave_ref, turn_ref, coarse_ref, fine_ref, sems = refs[5:]
    sub = lax.rem(lax.axis_index("ctx"), group)
    copies = [
        pltpu.make_async_copy(coarse_hbm.at[sub], coarse_ref, sems.at[0]),
        pltpu.make_async_copy(fine_hbm, fine_ref, sems.at[1]),
        pltpu.make_async_copy(left_hbm.at[sub], left_ref, sems.at[2]),
        pltpu.make_async_copy(wave_hbm, wave_ref, sems.at[3]),
        pltpu.make_async_copy(back_hbm.at[sub], back_ref, sems.at[4]),
    ]
    for copy in copies:
        copy.start()
    copies[0].wait()
    copies[1].wait()
    fine_re, fine_im = fine_ref[0], fine_ref[1]
    for number in range(coarse_ref.shape[1]):
        tab_re = coarse_ref[0, number : number + 1]
        tab_im = coarse_ref[1, number : number + 1]
        cut = slice(number * STEP, (number + 1) * STEP)
        turn_ref[0, cut] = fine_re * tab_re - fine_im * tab_im
        turn_ref[1, cut] = fine_re * tab_im + fine_im * tab_re
    for copy in copies[2:]:
        copy.wait()


def run_tables(group, tables):
    left, back, wave, coarse, fine = tables
    own = left.shape[1] // 2
    return pl.pallas_call(
        functools.partial(tables_kernel, group),
        out_shape=(
            jax.ShapeDtypeStruct(left.shape[1:], BF),
            jax.ShapeDtypeStruct(back.shape[1:], BF),
            jax.ShapeDtypeStruct(wave.shape, BF),
            jax.ShapeDtypeStruct((2, own, COLS), F32),
        ),
        in_specs=[HBM] * 5,
        out_specs=(VMEM,) * 4,
        scratch_shapes=[
            pltpu.VMEM(coarse.shape[1:], F32),
            pltpu.VMEM(fine.shape, F32),
            pltpu.SemaphoreType.DMA((5,)),
        ],
        compiler_params=params(40),
        cost_estimate=cost(3e9),
        name="load_tables",
    )(*tables)


def prepare_kernel(chans, group, *refs):
    filter_hbm, key_hbm, value_hbm = refs[:3]
    outs = refs[3 : 3 + chans]
    filter_ref, key_ref, value_ref, pair_ref, sems = refs[3 + chans :]
    home = lax.axis_index("ctx") // group
    rows = pair_ref.shape[2]
    step = rows // PIECES
    copies = []
    for number in range(PIECES):
        cut = slice(number * step * COLS, (number + 1) * step * COLS)
        for kind, (source, target) in enumerate(
            ((filter_hbm, filter_ref), (key_hbm, key_ref), (value_hbm, value_ref))
        ):
            copy = pltpu.make_async_copy(
                source.at[:, cut], target.at[:, cut], sems.at[kind, number]
            )
            copy.start()
            copies.append(copy)
    shape = (chans, 16, COLS)
    for number in range(PIECES):
        for copy in copies[3 * number : 3 * number + 3]:
            copy.wait()
        for first in range(number * step, (number + 1) * step, 16):
            cut = slice(first * COLS, (first + 16) * COLS)
            pair_ref[:, 0, first : first + 16] = filter_ref[:, cut].astype(BF).reshape(shape)
            signal = key_ref[:, cut].astype(F32) * value_ref[:, cut].astype(F32)
            pair_ref[:, 1, first : first + 16] = signal.astype(BF).reshape(shape)
    for rel in range(chans):
        outs[rel][...] = pair_ref[home ^ rel]


def run_prepare(long_filter, key, value, group):
    chans, tok_count = key.shape
    rows = tok_count // COLS
    return pl.pallas_call(
        functools.partial(prepare_kernel, chans, group),
        out_shape=(jax.ShapeDtypeStruct((2, rows, COLS), BF),) * chans,
        in_specs=[HBM] * 3,
        out_specs=(VMEM,) * chans,
        scratch_shapes=[
            pltpu.VMEM((chans, tok_count), F32),
            pltpu.VMEM((chans, tok_count), BF),
            pltpu.VMEM((chans, tok_count), BF),
            pltpu.VMEM((chans, 2, rows, COLS), BF),
            pltpu.SemaphoreType.DMA((3, PIECES)),
        ],
        compiler_params=params(60),
        cost_estimate=cost(4 * chans * tok_count),
        name="prepare_blocks",
    )(long_filter, key, value)


def finish_kernel(first_ref, acc_ref, got_ref, out_hbm, out_ref, sems):
    feats, rows, _ = first_ref.shape
    step = rows // PIECES
    copies = []
    for number in range(PIECES):
        for row in range(number * step, (number + 1) * step, 16):
            cut = slice(row, row + 16)
            second = (acc_ref[:, cut] + got_ref[:, cut].astype(F32)).astype(BF)
            whole = jnp.concatenate([first_ref[:, cut], second], 2)
            out_ref[:, row * COLS : (row + 16) * COLS] = whole.reshape(feats, 16 * COLS)
        cut = slice(number * step * COLS, (number + 1) * step * COLS)
        copy = pltpu.make_async_copy(out_ref.at[:, cut], out_hbm.at[:, cut], sems.at[number])
        copy.start()
        copies.append(copy)
    for copy in copies:
        copy.wait()


def run_finish(first, acc, got):
    feats, rows, _ = first.shape
    return pl.pallas_call(
        finish_kernel,
        out_shape=jax.ShapeDtypeStruct((feats, rows * COLS), BF),
        in_specs=[VMEM] * 3,
        out_specs=HBM,
        scratch_shapes=[
            pltpu.VMEM((feats, rows * COLS), BF),
            pltpu.SemaphoreType.DMA((PIECES,)),
        ],
        compiler_params=params(12),
        cost_estimate=cost(feats * rows * COLS),
        name="finish",
    )(first, acc, got)


def early_kernel(chans, group, early, late, *refs):
    count = len(early) * group
    blocks, (left_ref, sum_ref, rest_ref) = refs[:count], refs[count : count + 3]
    x_ref, part_ref = refs[count + 3 :]
    rows = blocks[0].shape[1]
    home = lax.axis_index("ctx") // group
    for rels, target in ((early, part_ref), (late, rest_ref)):
        for number in range(len(rels) * group):
            step, rel = number // len(rels), rels[number % len(rels)]
            first = pl.multiple_of((step * chans + (home ^ rel)) * rows, rows)
            target[:, number * rows : (number + 1) * rows] = left_ref[:, pl.ds(first, rows)]
    for number, block in enumerate(blocks):
        for kind in range(2):
            x_ref[kind, number * rows : (number + 1) * rows] = block[kind]
    half = sum_ref.shape[1] // 2
    for kind in range(2):
        for tile in range(0, COLS, 256):
            cut = slice(tile, tile + 256)
            sum_ref[kind, :half, cut] = dot(part_ref[:half], x_ref[kind, :, cut])
            sum_ref[kind, half:, cut] = dot(part_ref[half:], x_ref[kind, :, cut])


def run_early(blocks, chans, group, early, late, left):
    size, big = left.shape
    rows = big // (chans * group)
    width, rest = len(early) * group * rows, len(late) * group * rows
    return pl.pallas_call(
        functools.partial(early_kernel, chans, group, early, late),
        out_shape=(
            jax.ShapeDtypeStruct((2, size, COLS), F32),
            jax.ShapeDtypeStruct((size, rest), BF),
        ),
        in_specs=[VMEM] * (len(blocks) + 1),
        out_specs=(VMEM, VMEM),
        scratch_shapes=[pltpu.VMEM((2, width, COLS), BF), pltpu.VMEM((size, width), BF)],
        compiler_params=params(12),
        cost_estimate=cost(4 * size * COLS * width),
        name="early_stage",
    )(*blocks, left)


def spectrum_kernel(scale, *refs):
    count = len(refs) - 9
    blocks = refs[:count]
    sum_ref, left_ref, wave_ref, turn_ref, prod_ref, out_ref = refs[count : count + 6]
    x_ref, mid_ref, spec_ref = refs[count + 6 :]
    rows = blocks[0].shape[1]
    own = mid_ref.shape[0]
    for number, block in enumerate(blocks):
        for kind in range(2):
            x_ref[kind, number * rows : (number + 1) * rows] = block[kind]
    for kind in range(2):
        for tile in range(0, COLS, 256):
            cut = slice(tile, tile + 256)
            val_re = dot(left_ref[:own], x_ref[kind, :, cut]) + sum_ref[kind, :own, cut]
            val_im = dot(left_ref[own:], x_ref[kind, :, cut]) + sum_ref[kind, own:, cut]
            tab_re, tab_im = turn_ref[0, :, cut], turn_ref[1, :, cut]
            mid_re = (val_re * tab_re - val_im * tab_im).astype(BF)
            mid_ref[:, cut] = mid_re
            mid_ref[:, COLS + tile : COLS + tile + 256] = (
                val_re * tab_im + val_im * tab_re
            ).astype(BF)
            mid_ref[:, 2 * COLS + tile : 2 * COLS + tile + 256] = -mid_re
        for tile in range(0, COLS, 256):
            cut = slice(tile, tile + 256)
            out_re = dot(mid_ref[:, : 2 * COLS], wave_ref[:, cut])
            out_im = dot(mid_ref[:, COLS:], wave_ref[:, cut])
            if kind == 0:
                spec_ref[0, :, cut] = out_re * scale
                spec_ref[1, :, cut] = out_im * scale
            else:
                fil_re, fil_im = spec_ref[0, :, cut], spec_ref[1, :, cut]
                prod_im = (out_re * fil_im + out_im * fil_re).astype(BF)
                prod_ref[:, cut] = prod_im
                prod_ref[:, COLS + tile : COLS + tile + 256] = (
                    out_re * fil_re - out_im * fil_im
                ).astype(BF)
                prod_ref[:, 2 * COLS + tile : 2 * COLS + tile + 256] = -prod_im
    back_stage(CUTS[0], CUTS[1], prod_ref, wave_ref, turn_ref, out_ref)


def back_stage(low, high, prod_ref, wave_ref, turn_ref, out_ref):
    own = prod_ref.shape[0]
    cut = slice(low, high)
    val_im = dot(prod_ref[:, : 2 * COLS], wave_ref[:, cut])
    val_re = dot(prod_ref[:, COLS:], wave_ref[:, cut])
    tab_re, tab_im = turn_ref[0, :, cut], turn_ref[1, :, cut]
    out_ref[:own] = (val_re * tab_re + val_im * tab_im).astype(BF)
    out_ref[own:] = (val_im * tab_re - val_re * tab_im).astype(BF)


def position_kernel(chans, group, *refs):
    parts, table_ref = refs[:group], refs[group]
    outs, sum_ref = refs[group + 1 : group + 1 + chans], refs[group + 1 + chans]
    home = lax.axis_index("ctx") // group
    depth = parts[0].shape[0]
    total = dot(table_ref[:, :depth], parts[0][...])
    for step in range(1, group):
        total += dot(table_ref[:, step * depth : (step + 1) * depth], parts[step][...])
    sum_ref[...] = total.astype(BF)
    rows = outs[0].shape[0]
    for rel in range(chans):
        outs[rel][...] = sum_ref[pl.ds(pl.multiple_of((home ^ rel) * rows, rows), rows)]


def skip_kernel(query_ref, key_ref, value_ref, gain_ref, out_ref):
    for chan in range(query_ref.shape[0]):
        signal = key_ref[chan].astype(F32) * value_ref[chan].astype(F32)
        out_ref[chan] = gain_ref[chan] * signal


def run_skip(query, key, value, gain):
    return pl.pallas_call(
        skip_kernel,
        out_shape=jax.ShapeDtypeStruct(query.shape, F32),
        in_specs=[VMEM] * 3 + [SMEM],
        out_specs=VMEM,
        compiler_params=params(12),
        cost_estimate=cost(2 * query.size),
        name="skip_term",
    )(query, key, value, gain)


def gate_kernel(chans, group, low, high, *refs):
    parts = refs[:chans]
    query_ref, skip_ref, out_ref = refs[chans:]
    cut = slice(low, high)
    home = lax.axis_index("ctx") // group
    for rel in range(chans):
        chan = home ^ rel
        total = parts[rel][...].astype(F32) + skip_ref[chan, :, cut]
        out_ref[chan] = (query_ref[chan, :, cut].astype(F32) * total).astype(BF)


def run_spectrum(blocks, sums, left, tables, scale):
    _, _, wave, turn = tables
    own, width = left.shape[0] // 2, left.shape[1]
    return pl.pallas_call(
        functools.partial(spectrum_kernel, scale),
        out_shape=(
            jax.ShapeDtypeStruct((own, 3 * COLS), BF),
            jax.ShapeDtypeStruct((2 * own, CUTS[1] - CUTS[0]), BF),
        ),
        in_specs=[VMEM] * (len(blocks) + 4),
        out_specs=(VMEM, VMEM),
        scratch_shapes=[
            pltpu.VMEM((2, width, COLS), BF),
            pltpu.VMEM((own, 3 * COLS), BF),
            pltpu.VMEM((2, own, COLS), F32),
        ],
        compiler_params=params(20),
        cost_estimate=cost(8 * own * COLS * (width + 3 * COLS)),
        name="spectrum_product",
    )(*blocks, sums, left, wave, turn)


def run_back(prod, tables, low, high):
    _, _, wave, turn = tables
    own = prod.shape[0]
    return pl.pallas_call(
        functools.partial(back_stage, low, high),
        out_shape=jax.ShapeDtypeStruct((2 * own, high - low), BF),
        in_specs=[VMEM] * 3,
        out_specs=VMEM,
        compiler_params=params(12),
        cost_estimate=cost(8 * own * COLS * (high - low)),
        name="back_columns",
    )(prod, wave, turn)


def run_position(parts, chans, group, table):
    out_rows, depth = table.shape
    cols = parts[0].shape[1]
    rows = out_rows // chans
    return pl.pallas_call(
        functools.partial(position_kernel, chans, group),
        out_shape=(jax.ShapeDtypeStruct((rows, cols), BF),) * chans,
        in_specs=[VMEM] * (group + 1),
        out_specs=(VMEM,) * chans,
        scratch_shapes=[pltpu.VMEM((out_rows, cols), BF)],
        compiler_params=params(12),
        cost_estimate=cost(2 * out_rows * depth * cols),
        name="back_positions",
    )(*parts, table)


def run_gate(parts, query, skip, group, low, high):
    chans, rows, _ = query.shape
    return pl.pallas_call(
        functools.partial(gate_kernel, chans, group, low, high),
        out_shape=jax.ShapeDtypeStruct((chans, rows, high - low), BF),
        in_specs=[VMEM] * (chans + 2),
        out_specs=VMEM,
        compiler_params=params(12),
        cost_estimate=cost(4 * chans * rows * (high - low)),
        name="gate",
    )(*parts, query, skip)


def mix_kernel(chans, slots, outputs, plane_ref, weight_ref, *refs):
    count = len(slots)
    feats = refs[count].shape[0]

    @pl.loop(0, refs[0].shape[1] // 16)
    def _(index):
        rows = pl.ds(pl.multiple_of(index * 16, 16), 16)
        sums = [[None] * feats for _ in outputs]
        for slot, ref in zip(slots, refs[:count]):
            for chan in range(chans):
                value = ref[chan, rows].astype(F32)
                row = plane_ref[slot] * chans + chan
                for out, total in zip(outputs, sums):
                    for feat in range(feats):
                        term = value * weight_ref[row, plane_ref[out[0]] * feats + feat]
                        total[feat] = term if total[feat] is None else total[feat] + term
        for ref, total in zip(refs[count:], sums):
            for feat in range(feats):
                ref[feat, rows] = total[feat].astype(ref.dtype)


def run_mix(planes, weight, slots, outputs, values):
    chans, rows, cols = values[0].shape
    feats = weight.shape[1] // 4
    size = feats * rows * cols
    return pl.pallas_call(
        functools.partial(mix_kernel, chans, slots, outputs),
        out_shape=tuple(jax.ShapeDtypeStruct((feats, rows, cols), out[1]) for out in outputs),
        in_specs=[SMEM, SMEM] + [VMEM] * len(slots),
        out_specs=(VMEM,) * len(outputs),
        compiler_params=params(12),
        cost_estimate=cost(2 * chans * len(slots) * len(outputs) * size),
        name="mix_features",
    )(planes, weight, *values)


def line_mix(gated, out_weight):
    plane = lax.axis_index("tp")
    near = plane < 2
    planes = jnp.stack(
        [plane, jnp.where(near, 2, 1), jnp.where(near, 3, 0), jnp.where(near, 0, 3), plane ^ 1]
    ).astype(jnp.int32)
    own_at, mid_at, far_at, edge_at, pair_at = range(5)
    weight = out_weight.astype(F32)
    mix = functools.partial(run_mix, planes, weight)
    swapped, gathered = gated
    far = lax.ppermute(gathered, "tp", [(0, 2), (3, 1)])
    mid = lax.ppermute(gathered, "tp", [(1, 2), (2, 1)])
    pair = lax.ppermute(swapped, "tp", [(0, 1), (1, 0), (2, 3), (3, 2)])
    to_mid, to_far = mix((own_at, pair_at), ((mid_at, BF), (far_at, BF)), (swapped, pair))
    from_far = lax.ppermute(to_far, "tp", [(1, 3), (2, 0)])
    from_mid = lax.ppermute(to_mid, "tp", [(1, 2), (2, 1)])
    gathered, _ = lax.optimization_barrier((gathered, to_mid))
    edge = lax.ppermute(gathered, "tp", [(0, 1), (3, 2)])
    far, mid, to_mid, to_far = lax.optimization_barrier((far, mid, to_mid, to_far))
    (to_edge,) = mix((own_at, far_at, mid_at), ((edge_at, BF),), (gathered, far, mid))
    from_edge = lax.ppermute(to_edge, "tp", [(2, 3), (1, 0)])
    (acc_swapped,) = mix((own_at, pair_at), ((own_at, F32),), (swapped, pair))
    (acc_gathered,) = mix(
        (own_at, far_at, mid_at, edge_at), ((own_at, F32),), (gathered, far, mid, edge)
    )
    done = (acc_swapped + from_far.astype(F32) + from_mid.astype(F32)).astype(BF)
    done, acc_gathered = lax.optimization_barrier((done, acc_gathered))
    return run_finish(done, acc_gathered, from_edge)


def gather_mix(gated, out_weight):
    plane = lax.axis_index("tp")
    outs = out_weight.shape[1] // lax.axis_size("tp")
    own_cols = lax.dynamic_slice_in_dim(out_weight, plane * outs, outs, 1)
    mixed = [
        jnp.einsum(
            "co,crl->orl",
            own_cols,
            lax.all_gather(own, "tp", axis=0, tiled=True),
            preferred_element_type=F32,
        ).astype(BF)
        for own in gated
    ]
    return jnp.concatenate(mixed, 2).reshape(outs, -1)


def local(query_gate, key_branch, value_branch, long_filter, skip_gain, out_weight):
    ctx_count = lax.axis_size("ctx")
    chans, tok_count = query_gate.shape
    rows = tok_count // COLS
    group = ctx_count // chans
    length = ctx_count * tok_count
    shape = (chans, rows, COLS)
    tables = run_tables(group, make_tables(ctx_count, group, chans, rows))

    def swap(values):
        got = [values[0]]
        for rel in range(1, chans):
            pairs = [
                (group * chip + core, group * (chip ^ rel) + core)
                for chip in range(chans)
                for core in range(group)
            ]
            got.append(lax.ppermute(values[rel], "ctx", pairs))
        return got

    def shift(value, step):
        pairs = [
            (group * chip + core, group * chip + (core + step) % group)
            for chip in range(chans)
            for core in range(group)
        ]
        return lax.ppermute(value, "ctx", pairs)

    query = query_gate.reshape(shape)
    key = key_branch.reshape(shape)
    value = value_branch.reshape(shape)
    blocks = run_prepare(long_filter, key_branch, value_branch, group)
    blocks = swap(list(blocks))
    early = (0, chans - 1)
    late = tuple(range(1, chans - 1))
    skip = run_skip(query, key, value, skip_gain)
    blocks[-1], tables, query, skip = lax.optimization_barrier((blocks[-1], tables, query, skip))

    def share(rels, values):
        values = [values[rel] for rel in rels]
        return values + [shift(part, -step) for step in range(1, group) for part in values]

    sums, rest = run_early(share(early, blocks), chans, group, early, late, tables[0])
    blocks = share(late, blocks)
    spans = list(zip(CUTS[:-1], CUTS[1:]))
    prod, back = run_spectrum(blocks, sums, rest, tables, 1.0 / length)
    backs = [back] + [run_back(prod, tables, *span) for span in spans[1:]]
    places = []
    for back in backs:
        parts = [back] + [shift(back, -step) for step in range(1, group)]
        places.append(run_position(parts, chans, group, tables[1]))
    gated = []
    parts = swap(list(places[0]))
    for number, span in enumerate(spans):
        if number + 1 < len(spans):
            parts, _ = lax.optimization_barrier((parts, places[number + 1]))
        if number > 0:
            parts, gated[-1] = lax.optimization_barrier((parts, gated[-1]))
        gated.append(run_gate(parts, query, skip, group, *span))
        if number + 1 < len(spans):
            parts = swap(list(places[number + 1]))
    return (line_mix if lax.axis_size("tp") == 4 else gather_mix)(gated, out_weight)


def solution(mesh):
    placed = (P("tp", "ctx"), P("tp", "ctx"), P("tp", "ctx"), P("tp", "ctx"), P("tp"), P())
    return jax.shard_map(
        local, mesh=mesh, in_specs=placed, out_specs=P("tp", "ctx"), check_vma=False
    )
```

```python
import functools

import jax
import jax.numpy as jnp
import numpy as np
from jax import lax
from jax.experimental import pallas as pl
from jax.experimental.pallas import tpu as pltpu
from jax.sharding import PartitionSpec as P

COLS = 512
STEP = 32
PIECES = 4
CUTS = (0, 256, 512)
BF = jnp.bfloat16
F32 = jnp.float32
VMEM = pl.BlockSpec(memory_space=pltpu.VMEM)
SMEM = pl.BlockSpec(memory_space=pltpu.SMEM)
HBM = pl.BlockSpec(memory_space=pltpu.HBM)


def make_tables(ctx_count, group, chans, rows):
    big = ctx_count * rows
    own = big // group
    length = big * COLS
    k_one = np.arange(big, dtype=np.int64)
    n_one = np.arange(big, dtype=np.int64)
    angle = 2 * np.pi / (4 * big) * ((4 * k_one[:, None] + 1) * n_one[None, :] % (4 * big))
    both = np.stack([np.cos(angle), -np.sin(angle)], 0)
    both = both.reshape(2, group, own, chans, group, rows)
    left = np.empty((group, 2 * own, group, chans * rows))
    back_left = np.empty((group, chans * rows, group, 2 * own))
    for sub in range(group):
        for step in range(group):
            other = (sub + step) % group
            left[sub, :, step] = both[:, sub, :, :, other].reshape(2 * own, -1)
            back_left[sub, :, step] = both[:, other, :, :, sub].reshape(2 * own, -1).T
    n_two = np.arange(COLS, dtype=np.int64)
    coarse = STEP * np.arange(big // STEP, dtype=np.int64)
    fine = np.arange(STEP, dtype=np.int64)
    angle = 2 * np.pi / (4 * length) * (4 * coarse[:, None] * n_two[None, :] % (4 * length))
    coarse = np.stack([np.cos(angle), -np.sin(angle)], 0).reshape(2, group, own // STEP, COLS)
    coarse = np.ascontiguousarray(coarse.transpose(1, 0, 2, 3))
    angle = 2 * np.pi / (4 * length) * ((4 * fine[:, None] + 1) * n_two[None, :] % (4 * length))
    fine = np.stack([np.cos(angle), -np.sin(angle)], 0)
    angle = 2 * np.pi / COLS * (n_two[:, None] * n_two[None, :] % COLS)
    return (
        left.reshape(group, 2 * own, big).astype(BF),
        back_left.reshape(group, chans * rows, 2 * big).astype(BF),
        np.concatenate([np.cos(angle), np.sin(angle)], 0).astype(BF),
        coarse.astype(np.float32),
        fine.astype(np.float32),
    )


def dot(left, right):
    return jnp.dot(left, right, preferred_element_type=F32)


def cost(flops):
    return pl.CostEstimate(flops=int(flops), bytes_accessed=0, transcendentals=0)


def params(mib):
    return pltpu.CompilerParams(vmem_limit_bytes=mib * 2**20)


def tables_kernel(group, *refs):
    left_hbm, back_hbm, wave_hbm, coarse_hbm, fine_hbm = refs[:5]
    left_ref, back_ref, wave_ref, turn_ref, coarse_ref, fine_ref, sems = refs[5:]
    sub = lax.rem(lax.axis_index("ctx"), group)
    copies = [
        pltpu.make_async_copy(coarse_hbm.at[sub], coarse_ref, sems.at[0]),
        pltpu.make_async_copy(fine_hbm, fine_ref, sems.at[1]),
        pltpu.make_async_copy(left_hbm.at[sub], left_ref, sems.at[2]),
        pltpu.make_async_copy(wave_hbm, wave_ref, sems.at[3]),
        pltpu.make_async_copy(back_hbm.at[sub], back_ref, sems.at[4]),
    ]
    for copy in copies:
        copy.start()
    copies[0].wait()
    copies[1].wait()
    fine_re, fine_im = fine_ref[0], fine_ref[1]
    for number in range(coarse_ref.shape[1]):
        tab_re = coarse_ref[0, number : number + 1]
        tab_im = coarse_ref[1, number : number + 1]
        cut = slice(number * STEP, (number + 1) * STEP)
        turn_ref[0, cut] = fine_re * tab_re - fine_im * tab_im
        turn_ref[1, cut] = fine_re * tab_im + fine_im * tab_re
    for copy in copies[2:]:
        copy.wait()


def run_tables(group, tables):
    left, back, wave, coarse, fine = tables
    own = left.shape[1] // 2
    return pl.pallas_call(
        functools.partial(tables_kernel, group),
        out_shape=(
            jax.ShapeDtypeStruct(left.shape[1:], BF),
            jax.ShapeDtypeStruct(back.shape[1:], BF),
            jax.ShapeDtypeStruct(wave.shape, BF),
            jax.ShapeDtypeStruct((2, own, COLS), F32),
        ),
        in_specs=[HBM] * 5,
        out_specs=(VMEM,) * 4,
        scratch_shapes=[
            pltpu.VMEM(coarse.shape[1:], F32),
            pltpu.VMEM(fine.shape, F32),
            pltpu.SemaphoreType.DMA((5,)),
        ],
        compiler_params=params(40),
        cost_estimate=cost(3e9),
        name="load_tables",
    )(*tables)


def prepare_kernel(chans, group, *refs):
    filter_hbm, key_hbm, value_hbm = refs[:3]
    outs = refs[3 : 3 + chans]
    filter_ref, key_ref, value_ref, pair_ref, sems = refs[3 + chans :]
    home = lax.axis_index("ctx") // group
    rows = pair_ref.shape[2]
    step = rows // PIECES
    copies = []
    for number in range(PIECES):
        cut = slice(number * step * COLS, (number + 1) * step * COLS)
        for kind, (source, target) in enumerate(
            ((filter_hbm, filter_ref), (key_hbm, key_ref), (value_hbm, value_ref))
        ):
            copy = pltpu.make_async_copy(
                source.at[:, cut], target.at[:, cut], sems.at[kind, number]
            )
            copy.start()
            copies.append(copy)
    shape = (chans, 16, COLS)
    for number in range(PIECES):
        for copy in copies[3 * number : 3 * number + 3]:
            copy.wait()
        for first in range(number * step, (number + 1) * step, 16):
            cut = slice(first * COLS, (first + 16) * COLS)
            pair_ref[:, 0, first : first + 16] = filter_ref[:, cut].astype(BF).reshape(shape)
            signal = key_ref[:, cut].astype(F32) * value_ref[:, cut].astype(F32)
            pair_ref[:, 1, first : first + 16] = signal.astype(BF).reshape(shape)
    for rel in range(chans):
        outs[rel][...] = pair_ref[home ^ rel]


def run_prepare(long_filter, key, value, group):
    chans, tok_count = key.shape
    rows = tok_count // COLS
    return pl.pallas_call(
        functools.partial(prepare_kernel, chans, group),
        out_shape=(jax.ShapeDtypeStruct((2, rows, COLS), BF),) * chans,
        in_specs=[HBM] * 3,
        out_specs=(VMEM,) * chans,
        scratch_shapes=[
            pltpu.VMEM((chans, tok_count), F32),
            pltpu.VMEM((chans, tok_count), BF),
            pltpu.VMEM((chans, tok_count), BF),
            pltpu.VMEM((chans, 2, rows, COLS), BF),
            pltpu.SemaphoreType.DMA((3, PIECES)),
        ],
        compiler_params=params(60),
        cost_estimate=cost(4 * chans * tok_count),
        name="prepare_blocks",
    )(long_filter, key, value)


def finish_kernel(first_ref, acc_ref, got_ref, out_hbm, out_ref, sems):
    feats, rows, _ = first_ref.shape
    step = rows // PIECES
    copies = []
    for number in range(PIECES):
        for row in range(number * step, (number + 1) * step, 16):
            cut = slice(row, row + 16)
            second = (acc_ref[:, cut] + got_ref[:, cut].astype(F32)).astype(BF)
            whole = jnp.concatenate([first_ref[:, cut], second], 2)
            out_ref[:, row * COLS : (row + 16) * COLS] = whole.reshape(feats, 16 * COLS)
        cut = slice(number * step * COLS, (number + 1) * step * COLS)
        copy = pltpu.make_async_copy(out_ref.at[:, cut], out_hbm.at[:, cut], sems.at[number])
        copy.start()
        copies.append(copy)
    for copy in copies:
        copy.wait()


def run_finish(first, acc, got):
    feats, rows, _ = first.shape
    return pl.pallas_call(
        finish_kernel,
        out_shape=jax.ShapeDtypeStruct((feats, rows * COLS), BF),
        in_specs=[VMEM] * 3,
        out_specs=HBM,
        scratch_shapes=[
            pltpu.VMEM((feats, rows * COLS), BF),
            pltpu.SemaphoreType.DMA((PIECES,)),
        ],
        compiler_params=params(12),
        cost_estimate=cost(feats * rows * COLS),
        name="finish",
    )(first, acc, got)


def early_kernel(chans, group, early, late, *refs):
    count = len(early) * group
    blocks, (left_ref, sum_ref, rest_ref) = refs[:count], refs[count : count + 3]
    x_ref, part_ref = refs[count + 3 :]
    rows = blocks[0].shape[1]
    home = lax.axis_index("ctx") // group
    for rels, target in ((early, part_ref), (late, rest_ref)):
        for number in range(len(rels) * group):
            step, rel = number // len(rels), rels[number % len(rels)]
            first = pl.multiple_of((step * chans + (home ^ rel)) * rows, rows)
            target[:, number * rows : (number + 1) * rows] = left_ref[:, pl.ds(first, rows)]
    for number, block in enumerate(blocks):
        for kind in range(2):
            x_ref[kind, number * rows : (number + 1) * rows] = block[kind]
    half = sum_ref.shape[1] // 2
    for kind in range(2):
        for tile in range(0, COLS, 256):
            cut = slice(tile, tile + 256)
            sum_ref[kind, :half, cut] = dot(part_ref[:half], x_ref[kind, :, cut])
            sum_ref[kind, half:, cut] = dot(part_ref[half:], x_ref[kind, :, cut])


def run_early(blocks, chans, group, early, late, left):
    size, big = left.shape
    rows = big // (chans * group)
    width, rest = len(early) * group * rows, len(late) * group * rows
    return pl.pallas_call(
        functools.partial(early_kernel, chans, group, early, late),
        out_shape=(
            jax.ShapeDtypeStruct((2, size, COLS), F32),
            jax.ShapeDtypeStruct((size, rest), BF),
        ),
        in_specs=[VMEM] * (len(blocks) + 1),
        out_specs=(VMEM, VMEM),
        scratch_shapes=[pltpu.VMEM((2, width, COLS), BF), pltpu.VMEM((size, width), BF)],
        compiler_params=params(12),
        cost_estimate=cost(4 * size * COLS * width),
        name="early_stage",
    )(*blocks, left)


def spectrum_kernel(scale, *refs):
    count = len(refs) - 9
    blocks = refs[:count]
    sum_ref, left_ref, wave_ref, turn_ref, prod_ref, out_ref = refs[count : count + 6]
    x_ref, mid_ref, spec_ref = refs[count + 6 :]
    rows = blocks[0].shape[1]
    own = mid_ref.shape[0]
    for number, block in enumerate(blocks):
        for kind in range(2):
            x_ref[kind, number * rows : (number + 1) * rows] = block[kind]
    for kind in range(2):
        for tile in range(0, COLS, 256):
            cut = slice(tile, tile + 256)
            val_re = dot(left_ref[:own], x_ref[kind, :, cut]) + sum_ref[kind, :own, cut]
            val_im = dot(left_ref[own:], x_ref[kind, :, cut]) + sum_ref[kind, own:, cut]
            tab_re, tab_im = turn_ref[0, :, cut], turn_ref[1, :, cut]
            mid_re = (val_re * tab_re - val_im * tab_im).astype(BF)
            mid_ref[:, cut] = mid_re
            mid_ref[:, COLS + tile : COLS + tile + 256] = (
                val_re * tab_im + val_im * tab_re
            ).astype(BF)
            mid_ref[:, 2 * COLS + tile : 2 * COLS + tile + 256] = -mid_re
        for tile in range(0, COLS, 256):
            cut = slice(tile, tile + 256)
            out_re = dot(mid_ref[:, : 2 * COLS], wave_ref[:, cut])
            out_im = dot(mid_ref[:, COLS:], wave_ref[:, cut])
            if kind == 0:
                spec_ref[0, :, cut] = out_re * scale
                spec_ref[1, :, cut] = out_im * scale
            else:
                fil_re, fil_im = spec_ref[0, :, cut], spec_ref[1, :, cut]
                prod_im = (out_re * fil_im + out_im * fil_re).astype(BF)
                prod_ref[:, cut] = prod_im
                prod_ref[:, COLS + tile : COLS + tile + 256] = (
                    out_re * fil_re - out_im * fil_im
                ).astype(BF)
                prod_ref[:, 2 * COLS + tile : 2 * COLS + tile + 256] = -prod_im
    back_stage(CUTS[0], CUTS[1], prod_ref, wave_ref, turn_ref, out_ref)


def back_stage(low, high, prod_ref, wave_ref, turn_ref, out_ref):
    own = prod_ref.shape[0]
    cut = slice(low, high)
    val_im = dot(prod_ref[:, : 2 * COLS], wave_ref[:, cut])
    val_re = dot(prod_ref[:, COLS:], wave_ref[:, cut])
    tab_re, tab_im = turn_ref[0, :, cut], turn_ref[1, :, cut]
    out_ref[:own] = (val_re * tab_re + val_im * tab_im).astype(BF)
    out_ref[own:] = (val_im * tab_re - val_re * tab_im).astype(BF)


def position_kernel(chans, group, *refs):
    parts, table_ref = refs[:group], refs[group]
    outs, sum_ref = refs[group + 1 : group + 1 + chans], refs[group + 1 + chans]
    home = lax.axis_index("ctx") // group
    depth = parts[0].shape[0]
    total = dot(table_ref[:, :depth], parts[0][...])
    for step in range(1, group):
        total += dot(table_ref[:, step * depth : (step + 1) * depth], parts[step][...])
    sum_ref[...] = total.astype(BF)
    rows = outs[0].shape[0]
    for rel in range(chans):
        outs[rel][...] = sum_ref[pl.ds(pl.multiple_of((home ^ rel) * rows, rows), rows)]


def skip_kernel(query_ref, key_ref, value_ref, gain_ref, out_ref):
    for chan in range(query_ref.shape[0]):
        signal = key_ref[chan].astype(F32) * value_ref[chan].astype(F32)
        out_ref[chan] = gain_ref[chan] * signal


def run_skip(query, key, value, gain):
    return pl.pallas_call(
        skip_kernel,
        out_shape=jax.ShapeDtypeStruct(query.shape, F32),
        in_specs=[VMEM] * 3 + [SMEM],
        out_specs=VMEM,
        compiler_params=params(12),
        cost_estimate=cost(2 * query.size),
        name="skip_term",
    )(query, key, value, gain)


def gate_kernel(chans, group, low, high, *refs):
    parts = refs[:chans]
    query_ref, skip_ref, out_ref = refs[chans:]
    cut = slice(low, high)
    home = lax.axis_index("ctx") // group
    for rel in range(chans):
        chan = home ^ rel
        total = parts[rel][...].astype(F32) + skip_ref[chan, :, cut]
        out_ref[chan] = (query_ref[chan, :, cut].astype(F32) * total).astype(BF)


def run_spectrum(blocks, sums, left, tables, scale):
    _, _, wave, turn = tables
    own, width = left.shape[0] // 2, left.shape[1]
    return pl.pallas_call(
        functools.partial(spectrum_kernel, scale),
        out_shape=(
            jax.ShapeDtypeStruct((own, 3 * COLS), BF),
            jax.ShapeDtypeStruct((2 * own, CUTS[1] - CUTS[0]), BF),
        ),
        in_specs=[VMEM] * (len(blocks) + 4),
        out_specs=(VMEM, VMEM),
        scratch_shapes=[
            pltpu.VMEM((2, width, COLS), BF),
            pltpu.VMEM((own, 3 * COLS), BF),
            pltpu.VMEM((2, own, COLS), F32),
        ],
        compiler_params=params(20),
        cost_estimate=cost(8 * own * COLS * (width + 3 * COLS)),
        name="spectrum_product",
    )(*blocks, sums, left, wave, turn)


def run_back(prod, tables, low, high):
    _, _, wave, turn = tables
    own = prod.shape[0]
    return pl.pallas_call(
        functools.partial(back_stage, low, high),
        out_shape=jax.ShapeDtypeStruct((2 * own, high - low), BF),
        in_specs=[VMEM] * 3,
        out_specs=VMEM,
        compiler_params=params(12),
        cost_estimate=cost(8 * own * COLS * (high - low)),
        name="back_columns",
    )(prod, wave, turn)


def run_position(parts, chans, group, table):
    out_rows, depth = table.shape
    cols = parts[0].shape[1]
    rows = out_rows // chans
    return pl.pallas_call(
        functools.partial(position_kernel, chans, group),
        out_shape=(jax.ShapeDtypeStruct((rows, cols), BF),) * chans,
        in_specs=[VMEM] * (group + 1),
        out_specs=(VMEM,) * chans,
        scratch_shapes=[pltpu.VMEM((out_rows, cols), BF)],
        compiler_params=params(12),
        cost_estimate=cost(2 * out_rows * depth * cols),
        name="back_positions",
    )(*parts, table)


def run_gate(parts, query, skip, group, low, high):
    chans, rows, _ = query.shape
    return pl.pallas_call(
        functools.partial(gate_kernel, chans, group, low, high),
        out_shape=jax.ShapeDtypeStruct((chans, rows, high - low), BF),
        in_specs=[VMEM] * (chans + 2),
        out_specs=VMEM,
        compiler_params=params(12),
        cost_estimate=cost(4 * chans * rows * (high - low)),
        name="gate",
    )(*parts, query, skip)


def mix_kernel(chans, slots, outputs, plane_ref, weight_ref, *refs):
    count = len(slots)
    feats = refs[count].shape[0]

    @pl.loop(0, refs[0].shape[1] // 16, unroll=True)
    def _(index):
        rows = pl.ds(pl.multiple_of(index * 16, 16), 16)
        sums = [[None] * feats for _ in outputs]
        for slot, ref in zip(slots, refs[:count]):
            for chan in range(chans):
                value = ref[chan, rows].astype(F32)
                row = plane_ref[slot] * chans + chan
                for out, total in zip(outputs, sums):
                    for feat in range(feats):
                        term = value * weight_ref[row, plane_ref[out[0]] * feats + feat]
                        total[feat] = term if total[feat] is None else total[feat] + term
        for ref, total in zip(refs[count:], sums):
            for feat in range(feats):
                ref[feat, rows] = total[feat].astype(ref.dtype)


def run_mix(planes, weight, slots, outputs, values):
    chans, rows, cols = values[0].shape
    feats = weight.shape[1] // 4
    size = feats * rows * cols
    return pl.pallas_call(
        functools.partial(mix_kernel, chans, slots, outputs),
        out_shape=tuple(jax.ShapeDtypeStruct((feats, rows, cols), out[1]) for out in outputs),
        in_specs=[SMEM, SMEM] + [VMEM] * len(slots),
        out_specs=(VMEM,) * len(outputs),
        compiler_params=params(12),
        cost_estimate=cost(2 * chans * len(slots) * len(outputs) * size),
        name="mix_features",
    )(planes, weight, *values)


def line_mix(gated, out_weight):
    plane = lax.axis_index("tp")
    near = plane < 2
    planes = jnp.stack(
        [plane, jnp.where(near, 2, 1), jnp.where(near, 3, 0), jnp.where(near, 0, 3), plane ^ 1]
    ).astype(jnp.int32)
    own_at, mid_at, far_at, edge_at, pair_at = range(5)
    weight = out_weight.astype(F32)
    mix = functools.partial(run_mix, planes, weight)
    swapped, gathered = gated
    far = lax.ppermute(gathered, "tp", [(0, 2), (3, 1)])
    mid = lax.ppermute(gathered, "tp", [(1, 2), (2, 1)])
    pair = lax.ppermute(swapped, "tp", [(0, 1), (1, 0), (2, 3), (3, 2)])
    to_mid, to_far = mix((own_at, pair_at), ((mid_at, BF), (far_at, BF)), (swapped, pair))
    from_far = lax.ppermute(to_far, "tp", [(1, 3), (2, 0)])
    from_mid = lax.ppermute(to_mid, "tp", [(1, 2), (2, 1)])
    gathered, _ = lax.optimization_barrier((gathered, to_mid))
    edge = lax.ppermute(gathered, "tp", [(0, 1), (3, 2)])
    far, mid, to_mid, to_far = lax.optimization_barrier((far, mid, to_mid, to_far))
    (to_edge,) = mix((own_at, far_at, mid_at), ((edge_at, BF),), (gathered, far, mid))
    from_edge = lax.ppermute(to_edge, "tp", [(2, 3), (1, 0)])
    (acc_swapped,) = mix((own_at, pair_at), ((own_at, F32),), (swapped, pair))
    (acc_gathered,) = mix(
        (own_at, far_at, mid_at, edge_at), ((own_at, F32),), (gathered, far, mid, edge)
    )
    done = (acc_swapped + from_far.astype(F32) + from_mid.astype(F32)).astype(BF)
    done, acc_gathered = lax.optimization_barrier((done, acc_gathered))
    return run_finish(done, acc_gathered, from_edge)


def gather_mix(gated, out_weight):
    plane = lax.axis_index("tp")
    outs = out_weight.shape[1] // lax.axis_size("tp")
    own_cols = lax.dynamic_slice_in_dim(out_weight, plane * outs, outs, 1)
    mixed = [
        jnp.einsum(
            "co,crl->orl",
            own_cols,
            lax.all_gather(own, "tp", axis=0, tiled=True),
            preferred_element_type=F32,
        ).astype(BF)
        for own in gated
    ]
    return jnp.concatenate(mixed, 2).reshape(outs, -1)


def local(query_gate, key_branch, value_branch, long_filter, skip_gain, out_weight):
    ctx_count = lax.axis_size("ctx")
    chans, tok_count = query_gate.shape
    rows = tok_count // COLS
    group = ctx_count // chans
    length = ctx_count * tok_count
    shape = (chans, rows, COLS)
    tables = run_tables(group, make_tables(ctx_count, group, chans, rows))

    def swap(values):
        got = [values[0]]
        for rel in range(1, chans):
            pairs = [
                (group * chip + core, group * (chip ^ rel) + core)
                for chip in range(chans)
                for core in range(group)
            ]
            got.append(lax.ppermute(values[rel], "ctx", pairs))
        return got

    def shift(value, step):
        pairs = [
            (group * chip + core, group * chip + (core + step) % group)
            for chip in range(chans)
            for core in range(group)
        ]
        return lax.ppermute(value, "ctx", pairs)

    query = query_gate.reshape(shape)
    key = key_branch.reshape(shape)
    value = value_branch.reshape(shape)
    blocks = run_prepare(long_filter, key_branch, value_branch, group)
    blocks = swap(list(blocks))
    early = (0, chans - 1)
    late = tuple(range(1, chans - 1))
    skip = run_skip(query, key, value, skip_gain)
    blocks[-1], tables, query, skip = lax.optimization_barrier((blocks[-1], tables, query, skip))

    def share(rels, values):
        values = [values[rel] for rel in rels]
        return values + [shift(part, -step) for step in range(1, group) for part in values]

    sums, rest = run_early(share(early, blocks), chans, group, early, late, tables[0])
    blocks = share(late, blocks)
    spans = list(zip(CUTS[:-1], CUTS[1:]))
    prod, back = run_spectrum(blocks, sums, rest, tables, 1.0 / length)
    backs = [back] + [run_back(prod, tables, *span) for span in spans[1:]]
    places = []
    for back in backs:
        parts = [back] + [shift(back, -step) for step in range(1, group)]
        places.append(run_position(parts, chans, group, tables[1]))
    gated = []
    parts = swap(list(places[0]))
    for number, span in enumerate(spans):
        if number + 1 < len(spans):
            parts, _ = lax.optimization_barrier((parts, places[number + 1]))
        if number > 0:
            parts, gated[-1] = lax.optimization_barrier((parts, gated[-1]))
        gated.append(run_gate(parts, query, skip, group, *span))
        if number + 1 < len(spans):
            parts = swap(list(places[number + 1]))
    return (line_mix if lax.axis_size("tp") == 4 else gather_mix)(gated, out_weight)


def solution(mesh):
    placed = (P("tp", "ctx"), P("tp", "ctx"), P("tp", "ctx"), P("tp", "ctx"), P("tp"), P())
    return jax.shard_map(
        local, mesh=mesh, in_specs=placed, out_specs=P("tp", "ctx"), check_vma=False
    )
```
